128 devices in a mesh: row: 8 (over z, x_hi), col: 8 (over y, core), tm: 2 (over x_lo).
Axes of the slice: x: 4 (x_hi: 2, x_lo: 2; x = x_hi * 2 + x_lo), y: 4, z: 4, core: 2. Of those that a mesh axis runs over, the one named last changes fastest.
Arguments:
- tile_values: bfloat16 [8, 8, 2, 384, 128, 128], P('row', 'col', 'tm'), may hold values from -6 to 6
- tile_coords: int32 [8, 8, 2, 3, 384], P('row', 'col', 'tm'), may hold values from 0 to 31, as said below
- tile_counts: int32 [8, 8, 2], P('row', 'col', 'tm'), may hold values from 96 to 384, as said below
- factor_rows: bfloat16 [8, 2048, 256], P('row', ('col', 'tm')), may hold values from -0.23925781 to 0.23925781
- factor_cols: bfloat16 [8, 2048, 256], P('col', ('row', 'tm')), may hold values from -0.23925781 to 0.23925781
- factor_time: bfloat16 [64, 256], P('tm'), may hold values from -0.76953125 to 0.76953125
Outputs:
- grad_rows: float32 [8, 2048, 256], P('row', ('col', 'tm'))
- grad_cols: float32 [8, 2048, 256], P('col', ('row', 'tm'))
- grad_time: float32 [64, 256], P('tm')
The draws below stay inside these ranges and needn't reach their ends.
Inputs may be any that keep to these rules, and one draw needn't show every extreme that they name: `tile_coords`: on each device the 384 slots name distinct triples; row block below 16, column block below 16, snapshot below 32. Only the first tile_counts slots of a device are live; some device has all 384 live in every draw.
All inputs are finite; a program needn't handle non-finite values.
Results may differ from the reference program's by a relative error of at most 0.0003.
Values may be sent and summed in bfloat16 or wider, within the bound.
A program may use at most 128 MiB of HBM per device.

```python
import jax
import jax.numpy as jnp
from jax import lax

R = 256
TB = 128
K = 64
RB = 2048
CB = 2048
NT = 384
KS = 32
N_ROW = 8
N_COL = 8
N_TM = 2


def draw_tile_coords(key, part):
    key = jax.random.fold_in(key, 11)
    row_blocks = RB // TB
    col_blocks = CB // TB
    places = row_blocks * col_blocks * KS
    device_total = N_ROW * N_COL * N_TM
    device_keys = jax.random.split(key, device_total)
    chosen = jax.vmap(lambda subkey: jax.random.permutation(subkey, places)[:NT])(device_keys)
    chosen = chosen.astype(jnp.int32)
    row_block = chosen // (col_blocks * KS)
    col_block = chosen // KS % col_blocks
    snapshot = chosen % KS
    stacked = jnp.stack([row_block, col_block, snapshot], axis=1)
    return stacked.reshape(N_ROW, N_COL, N_TM, 3, NT).astype(jnp.int32)


def draw_tile_counts(key, part):
    key = jax.random.fold_in(key, 12)
    device_total = N_ROW * N_COL * N_TM
    first_key, second_key = jax.random.split(key)
    counted = jax.random.randint(first_key, (device_total,), NT // 4, NT + 1, dtype=jnp.int32)
    filled = jax.random.randint(second_key, (), 0, device_total, dtype=jnp.int32)
    counted = counted.at[filled].set(NT)
    return counted.reshape(N_ROW, N_COL, N_TM).astype(jnp.int32)


def block_scale(rng, dims, cuts, low, largest):
    factor_of = 1.0
    for axis_at, shards_of in cuts:
        heights = jax.random.uniform(jax.random.fold_in(jax.random.fold_in(rng, 6), axis_at), (shards_of,), jnp.float32, low / len(cuts), largest / len(cuts))
        factor_of = factor_of * jnp.repeat(jnp.exp(heights), dims[axis_at] // shards_of).reshape((-1,) + (1,) * (len(dims) - 1 - axis_at))
    return factor_of


def gaussian(own_key, extent, spread, limit, shards=(), held_as=jnp.bfloat16):
    drawn = spread * jax.random.normal(own_key, extent, jnp.float32)
    if shards:
        drawn = drawn * block_scale(own_key, extent, shards, -0.22, 0.18)
    return jnp.clip(drawn, -limit, limit).astype(held_as)


def setup_inputs(seed: int = 0) -> dict:
    key_of = jax.random.split(jax.random.key(seed), 7)
    return {
        "tile_values": gaussian(key_of[0], (N_ROW, N_COL, N_TM, NT, TB, TB), 1.0, 6.0, ((0, 8), (1, 8), (2, 2))),
        "tile_coords": draw_tile_coords(jax.random.fold_in(key_of[6], 71), 0),
        "tile_counts": draw_tile_counts(jax.random.fold_in(key_of[6], 71), 0),
        "factor_rows": gaussian(key_of[3], (N_ROW, RB, R), 0.04, 0.23925781, ((0, 8), (1, 16))),
        "factor_cols": gaussian(key_of[4], (N_COL, CB, R), 0.04, 0.23925781, ((0, 8), (1, 16))),
        "factor_time": gaussian(key_of[5], (K, R), 0.128, 0.76953125, ((0, 2),)),
    }


def reference(tile_values, tile_coords, tile_counts, factor_rows, factor_cols, factor_time):
    rank_width = factor_rows.shape[2]
    row_blocks = RB // TB
    col_blocks = CB // TB
    device_total = N_ROW * N_COL * N_TM
    row_tiles = factor_rows.reshape(N_ROW * row_blocks, TB, rank_width)
    col_tiles = factor_cols.reshape(N_COL * col_blocks, TB, rank_width)
    all_values = tile_values.reshape(device_total, NT, TB, TB)
    all_places = tile_coords.reshape(device_total, 3, NT)
    all_counts = tile_counts.reshape(device_total)
    device_ids = jnp.arange(device_total, dtype=jnp.int32)
    dev_rows = device_ids // (N_COL * N_TM)
    dev_cols = (device_ids // N_TM) % N_COL
    dev_times = device_ids % N_TM

    def per_device(totals, device_item):
        sum_rows, sum_cols, sum_time = totals
        tile_vals, tile_place, live_count, dev_row, dev_col, dev_time = device_item
        live_slots = jnp.arange(NT, dtype=jnp.int32) < live_count
        tile_vals = jnp.where(live_slots[:, None, None], tile_vals, jnp.zeros((), jnp.bfloat16))
        glob_row = (dev_row * row_blocks + tile_place[0]).astype(jnp.int32)
        glob_col = (dev_col * col_blocks + tile_place[1]).astype(jnp.int32)
        glob_snap = (dev_time * KS + tile_place[2]).astype(jnp.int32)
        row_take = row_tiles[glob_row].astype(jnp.float32)
        col_take = col_tiles[glob_col].astype(jnp.float32)
        time_take = factor_time[glob_snap].astype(jnp.float32)[:, None, :]
        float_vals = tile_vals.astype(jnp.float32)
        prod_cols = jnp.einsum("nij,njr->nir", float_vals, col_take)
        prod_rows = jnp.einsum("nij,nir->njr", float_vals, row_take)
        sum_rows = sum_rows.at[glob_row].add(prod_cols * time_take)
        sum_cols = sum_cols.at[glob_col].add(prod_rows * time_take)
        sum_time = sum_time.at[glob_snap].add(jnp.sum(row_take * prod_cols, axis=1))
        return (sum_rows, sum_cols, sum_time), None

    init_sums = (jnp.zeros(row_tiles.shape, jnp.float32), jnp.zeros(col_tiles.shape, jnp.float32), jnp.zeros((K, rank_width), jnp.float32))
    (sum_rows, sum_cols, sum_time), unused = lax.scan(per_device, init_sums, (all_values, all_places, all_counts, dev_rows, dev_cols, dev_times))
    flat_rows = factor_rows.reshape(-1, rank_width)
    flat_cols = factor_cols.reshape(-1, rank_width)
    gram_rows = jnp.dot(flat_rows.T, flat_rows, preferred_element_type=jnp.float32)
    gram_cols = jnp.dot(flat_cols.T, flat_cols, preferred_element_type=jnp.float32)
    gram_time = jnp.dot(factor_time.T, factor_time, preferred_element_type=jnp.float32)
    highest = lax.Precision.HIGHEST
    grad_rows = jnp.dot(flat_rows.astype(jnp.float32), gram_cols * gram_time, precision=highest) - sum_rows.reshape(-1, rank_width)
    grad_cols = jnp.dot(flat_cols.astype(jnp.float32), gram_rows * gram_time, precision=highest) - sum_cols.reshape(-1, rank_width)
    grad_time = jnp.dot(factor_time.astype(jnp.float32), gram_rows * gram_cols, precision=highest) - sum_time
    return grad_rows.reshape(N_ROW, RB, rank_width), grad_cols.reshape(N_COL, CB, rank_width), grad_time
```

```python
import jax
import jax.numpy as jnp
from jax import lax
from jax.experimental import pallas as pl
from jax.experimental.pallas import tpu as pltpu
from jax.sharding import PartitionSpec as P

F32 = jnp.float32
BF16 = jnp.bfloat16
I16 = jnp.int16
MESH = pl.DeviceIdType.MESH
EDGE = 128
RANK = 256
PAD = 16


class Net:
    def __init__(self, send, recv):
        self.send, self.recv, self.used, self.open = send, recv, 0, []

    def copy(self, src, dst, device):
        made = pltpu.make_async_remote_copy(
            src_ref=src,
            dst_ref=dst,
            send_sem=self.send.at[self.used],
            recv_sem=self.recv.at[self.used],
            device_id=device,
            device_id_type=MESH,
        )
        self.used += 1
        made.start()
        self.open.append(made)
        return made

    def close(self):
        for made in self.open:
            made.wait_send()


class Place:
    def __init__(self):
        row, col, self.t = lax.axis_index("row"), lax.axis_index("col"), lax.axis_index("tm")
        self.z, self.y, self.core = row // 2, col // 2, col % 2
        self.x = (row % 2) * 2 + self.t

    def at(self, dz=0, dy=0, dx=0, other=False):
        z, y, x = (self.z + dz) % 4, (self.y + dy) % 4, (self.x + dx) % 4
        core = 1 - self.core if other else self.core
        return (z * 2 + x // 2, y * 2 + core, x % 2)

    def pair(self):
        return (self.z * 2 + self.x // 2, self.y * 2 + self.core, 1 - self.t)

    def greet(self):
        barrier = pltpu.get_barrier_semaphore()
        others = [self.at(other=True)]
        for step in (1, 2, 3):
            others += [self.at(dz=step), self.at(dy=step), self.at(dx=step)]
        for device in others:
            pl.semaphore_signal(barrier, inc=1, device_id=device, device_id_type=MESH)
        pl.semaphore_wait(barrier, len(others))


def drive(*runs):
    runs = list(runs)
    while runs:
        for run in list(runs):
            if next(run, None) is None:
                runs.remove(run)


def ring_gather(net, view, half, me, plus, minus):
    up = net.copy(view(me), view(me), plus)
    down = net.copy(view(me), view(me), minus)
    yield 1
    before, after = (me + 3) % 4, (me + 1) % 4
    up.wait_recv()
    up = net.copy(half(before, 0), half(before, 0), plus)
    down.wait_recv()
    down = net.copy(half(after, 1), half(after, 1), minus)
    yield 1
    up.wait_recv()
    down.wait_recv()


def spread(net, view, me, devices):
    made = [net.copy(view(me), view(me), device) for device in devices]
    yield 1
    for copy in made:
        copy.wait_recv()


def swap(net, src, dst, device):
    made = net.copy(src, dst, device)
    yield 1
    made.wait_recv()


def encode(wire, value):
    rows = value.shape[0]
    top = jnp.max(jnp.abs(value), axis=0, keepdims=True)
    power = jnp.ceil(jnp.log2(jnp.maximum(top, 1e-30)))
    coded = jnp.clip(value * jnp.exp2(15.0 - power), -32767.0, 32767.0)
    wire[0:rows] = jnp.round(coded).astype(jnp.int32).astype(I16)
    wire[rows : rows + PAD] = jnp.broadcast_to(power, (PAD, RANK)).astype(jnp.int32).astype(I16)


def decode(wire):
    rows = wire.shape[0] - PAD
    power = wire[rows : rows + PAD].astype(jnp.int32).astype(F32)[0:1]
    return wire[0:rows].astype(jnp.int32).astype(F32) * jnp.exp2(power - 15.0)


def ring_reduce(net, src, me, plus, minus, sent, got, out):
    after, far, before = (me + 1) % 4, (me + 2) % 4, (me + 3) % 4
    encode(sent.at[0], src(far, 0))
    relay_up = net.copy(sent.at[0], got.at[0], plus)
    encode(sent.at[1], src(far, 1))
    relay_down = net.copy(sent.at[1], got.at[1], minus)
    encode(sent.at[2], src(after, 1))
    own_up = net.copy(sent.at[2], got.at[2], plus)
    encode(sent.at[3], src(before, 0))
    own_down = net.copy(sent.at[3], got.at[3], minus)
    yield 1
    relay_up.wait_recv()
    encode(sent.at[4], decode(got.at[0]) + src(after, 0))
    sum_up = net.copy(sent.at[4], got.at[4], plus)
    relay_down.wait_recv()
    encode(sent.at[5], decode(got.at[1]) + src(before, 1))
    sum_down = net.copy(sent.at[5], got.at[5], minus)
    yield 1
    for copy in (own_up, own_down, sum_up, sum_down):
        copy.wait_recv()
    out(0, src(me, 0) + decode(got.at[4]) + decode(got.at[3]))
    out(1, src(me, 1) + decode(got.at[2]) + decode(got.at[5]))


def gather_rows(net, at, full):
    yield from swap(net, full.at[at.y, at.core, at.t], full.at[at.y, at.core, at.t], at.pair())
    yield from ring_gather(
        net,
        lambda p: full.at[p, at.core],
        lambda p, h: full.at[p, at.core, h],
        at.y,
        at.at(dy=1),
        at.at(dy=3),
    )
    yield from swap(net, full.at[:, at.core], full.at[:, at.core], at.at(other=True))


def gather_cols_low(net, at, full):
    yield from ring_gather(
        net,
        lambda p: full.at[p, at.x, 0:64],
        lambda p, h: full.at[p, at.x, 32 * h : 32 * h + 32],
        at.z,
        at.at(dz=1),
        at.at(dz=3),
    )
    yield from ring_gather(
        net,
        lambda p: full.at[:, p, 0:64],
        lambda p, h: full.at[2 * h : 2 * h + 2, p, 0:64],
        at.x,
        at.at(dx=1),
        at.at(dx=3),
    )


def gather_cols_high(net, at, full):
    yield from ring_gather(
        net,
        lambda p: full.at[at.z, p, 64:128],
        lambda p, h: full.at[at.z, p, 64 + 32 * h : 96 + 32 * h],
        at.x,
        at.at(dx=1),
        at.at(dx=3),
    )
    yield from ring_gather(
        net,
        lambda p: full.at[p, :, 64:128],
        lambda p, h: full.at[p, 2 * h : 2 * h + 2, 64:128],
        at.z,
        at.at(dz=1),
        at.at(dz=3),
    )


def gather_kernel(rows, cols, times, a_full, b_full, c_full, send, recv):
    at = Place()
    net = Net(send, recv)
    a_full[at.y, at.core, at.t] = rows[0]
    b_full[at.z, at.x] = cols[0]
    c_full[at.t] = times[...]
    at.greet()
    drive(
        gather_cols_low(net, at, b_full),
        gather_cols_high(net, at, b_full),
        gather_rows(net, at, a_full),
        swap(net, c_full.at[at.t], c_full.at[at.t], at.pair()),
    )
    net.close()


LOADS = 12
UNROLL = 4


def tile_kernel(coords, count, values, a, b, times, sum_a, sum_b, sum_c, held, ctime, sems):
    slots = values.shape[0]
    part = slots // LOADS

    def load(i):
        span = pl.ds(i * part, part)
        return pltpu.make_async_copy(values.at[span], held.at[span], sems.at[i])

    for i in range(LOADS):
        load(i).start()
    sum_a[...] = jnp.zeros_like(sum_a)
    sum_b[...] = jnp.zeros_like(sum_b)
    sum_c[...] = jnp.zeros_like(sum_c)
    ctime[...] = times[...].astype(F32)
    live = count[0]

    def one(s):
        row, col, snap = coords[0, s], coords[1, s], coords[2, s]
        tile = held[s]
        a_here = a[row]
        prod = jnp.dot(tile, b[col], preferred_element_type=F32)
        back = lax.dot_general(tile, a_here, (((0,), (0,)), ((), ())), preferred_element_type=F32)
        scale = jnp.where(s < live, ctime[pl.ds(snap, 1), :], 0.0)
        mask = jnp.where(s < live, 1.0, 0.0)
        here = jnp.sum(a_here.astype(F32) * prod, axis=0, keepdims=True) * mask
        return row, col, snap, prod * scale, back * scale, here

    for i in range(LOADS):
        load(i).wait()

        @pl.loop(i * part, (i + 1) * part, step=UNROLL)
        def _(first):
            found = [one(first + u) for u in range(UNROLL)]
            for row, col, snap, to_row, to_col, here in found:
                sum_a[row] += to_row
                sum_b[col] += to_col
                sum_c[pl.ds(snap, 1), :] += here


def reduce_rows(net, at, part, chip, pair_sum, total, core_s, core_r, y_s, y_r, x_s, x_r):
    made = []
    order = [(at.y + step) % 4 for step in (2, 1, 3, 0)]
    for p in order:
        for h in range(2):
            encode(core_s.at[p, h], part[p, 1 - at.core, h])
        made.append(net.copy(core_s.at[p], core_r.at[p], at.at(other=True)))
    yield 1
    for p, copy in zip(order, made):
        copy.wait_recv()
        for h in range(2):
            chip[p, h] = part[p, at.core, h] + decode(core_r.at[p, h])

    def out(h, value):
        pair_sum[h] = value

    yield from ring_reduce(
        net, lambda p, h: chip[p, h], at.y, at.at(dy=1), at.at(dy=3), y_s, y_r, out
    )
    encode(x_s, pair_sum[1 - at.t])
    yield from swap(net, x_s, x_r, at.pair())
    total[...] = pair_sum[at.t] + decode(x_r)


def reduce_cols_low(net, at, part, mid, total, s1, r1, s2, r2):
    def out_mid(h, value):
        mid[2 * h : 2 * h + 2] = value.reshape(2, 64, RANK)

    def out(h, value):
        total[32 * h : 32 * h + 32] = value

    yield from ring_reduce(
        net,
        lambda p, h: part[2 * h : 2 * h + 2, p, 0:64].reshape(EDGE, RANK),
        at.x,
        at.at(dx=1),
        at.at(dx=3),
        s1,
        r1,
        out_mid,
    )
    yield from ring_reduce(
        net,
        lambda p, h: mid[p, 32 * h : 32 * h + 32],
        at.z,
        at.at(dz=1),
        at.at(dz=3),
        s2,
        r2,
        out,
    )


def reduce_cols_high(net, at, part, mid, total, s1, r1, s2, r2):
    def out_mid(h, value):
        mid[2 * h : 2 * h + 2] = value.reshape(2, 64, RANK)

    def out(h, value):
        total[64 + 32 * h : 96 + 32 * h] = value

    yield from ring_reduce(
        net,
        lambda p, h: part[p, 2 * h : 2 * h + 2, 64:128].reshape(EDGE, RANK),
        at.z,
        at.at(dz=1),
        at.at(dz=3),
        s1,
        r1,
        out_mid,
    )
    yield from ring_reduce(
        net,
        lambda p, h: mid[p, 32 * h : 32 * h + 32],
        at.x,
        at.at(dx=1),
        at.at(dx=3),
        s2,
        r2,
        out,
    )


def along(at, name):
    return [at.at(**{name: step}) for step in (1, 2, 3)]


def sum_four(ref):
    return (ref[0] + ref[1]) + (ref[2] + ref[3])


def gram_rows(net, at, whole, four, two, full):
    block = (at.y * 4 + at.core * 2 + at.t) * 16
    four[at.z] = whole[pl.ds(pl.multiple_of(block, 16), 16), :]
    yield from spread(net, lambda p: four.at[p], at.z, along(at, "dz"))
    two[0] = sum_four(four)
    yield from swap(net, two.at[0], two.at[1], at.at(dx=2))
    full[at.y, at.core, at.t] = two[0] + two[1]
    yield from swap(net, full.at[at.y, at.core, at.t], full.at[at.y, at.core, at.t], at.pair())
    yield from spread(net, lambda p: full.at[p, at.core], at.y, along(at, "dy"))
    yield from swap(net, full.at[:, at.core], full.at[:, at.core], at.at(other=True))


def gram_cols(net, at, whole, four, two, full):
    block = (at.z * 4 + at.x) * 16
    four[at.y] = whole[pl.ds(pl.multiple_of(block, 16), 16), :]
    yield from spread(net, lambda p: four.at[p], at.y, along(at, "dy"))
    two[0] = sum_four(four)
    yield from swap(net, two.at[0], two.at[1], at.at(other=True))
    full[at.z, at.x] = two[0] + two[1]
    yield from spread(net, lambda p: full.at[p, at.x], at.z, along(at, "dz"))
    yield from spread(net, lambda p: full.at[:, p], at.x, along(at, "dx"))


def reduce_time(net, at, part, four_y, two_y, four_z, two_z, total):
    four_y[at.y] = part[...]
    yield from spread(net, lambda p: four_y.at[p], at.y, along(at, "dy"))
    two_y[0] = sum_four(four_y)
    yield from swap(net, two_y.at[0], two_y.at[1], at.at(other=True))
    four_z[at.z] = two_y[0] + two_y[1]
    yield from spread(net, lambda p: four_z.at[p], at.z, along(at, "dz"))
    two_z[0] = sum_four(four_z)
    yield from swap(net, two_z.at[0], two_z.at[1], at.at(dx=2))
    total[...] = two_z[0] + two_z[1]


def exact_dot(left, right):
    high = right.astype(BF16)
    rest = right - high.astype(F32)
    mid = rest.astype(BF16)
    low = (rest - mid.astype(F32)).astype(BF16)
    return (
        jnp.dot(left, low, preferred_element_type=F32)
        + jnp.dot(left, mid, preferred_element_type=F32)
        + jnp.dot(left, high, preferred_element_type=F32)
    )


def gram(ref):
    block = ref[...]
    return lax.dot_general(block, block, (((0,), (0,)), ((), ())), preferred_element_type=F32)


def reduce_kernel(
    sum_a, sum_b, sum_c, a_full, b_full, c_full, grad_a, grad_b, grad_c, s, send, recv
):
    at = Place()
    net = Net(send, recv)
    a_flat = a_full.reshape(16, EDGE, RANK)
    b_flat = b_full.reshape(16, EDGE, RANK)
    at.greet()
    runs = [
        reduce_rows(
            net, at, sum_a, s["chip"], s["pair"], s["total_a"],
            s["core_s"], s["core_r"], s["y_s"], s["y_r"], s["x_s"], s["x_r"],
        ),
        reduce_cols_low(
            net, at, sum_b, s["mid0"], s["total_b"], s["l1_s"], s["l1_r"], s["l2_s"], s["l2_r"]
        ),
        reduce_cols_high(
            net, at, sum_b, s["mid1"], s["total_b"], s["h1_s"], s["h1_r"], s["h2_s"], s["h2_r"]
        ),
    ]
    for run in runs:
        next(run)
    s["gram_a"][...] = jnp.zeros((RANK, RANK), F32)
    s["gram_b"][...] = jnp.zeros((RANK, RANK), F32)

    @pl.loop(0, 16)
    def _(i):
        s["gram_a"][...] += gram(a_flat.at[i])
        s["gram_b"][...] += gram(b_flat.at[i])

    runs += [
        gram_rows(net, at, s["gram_a"], s["ga4"], s["ga2"], s["ga"]),
        gram_cols(net, at, s["gram_b"], s["gb4"], s["gb2"], s["gb"]),
        reduce_time(net, at, sum_c, s["cy4"], s["cy2"], s["cz4"], s["cz2"], s["total_c"]),
    ]
    drive(*runs)
    whole_a = s["ga"][...].reshape(RANK, RANK)
    whole_b = s["gb"][...].reshape(RANK, RANK)
    c_all = c_full[...].reshape(2 * c_full.shape[1], RANK)
    whole_c = lax.dot_general(c_all, c_all, (((0,), (0,)), ((), ())), preferred_element_type=F32)
    grad_a[0] = exact_dot(a_full[at.y, at.core, at.t], whole_b * whole_c) - s["total_a"][...]
    grad_b[0] = exact_dot(b_full[at.z, at.x], whole_a * whole_c) - s["total_b"][...]
    grad_c[...] = exact_dot(c_full[at.t], whole_a * whole_b) - s["total_c"][...]
    net.close()


def vmem(count):
    return [pl.BlockSpec(memory_space=pltpu.VMEM)] * count


def on_device(tile_values, tile_coords, tile_counts, factor_rows, factor_cols, factor_time):
    values = tile_values[0, 0, 0]
    coords = tile_coords[0, 0, 0]
    count = tile_counts.reshape(1)
    section = factor_time.shape[0]
    slots = values.shape[0]
    sds = jax.ShapeDtypeStruct
    copies = 32
    a_full, b_full, c_full = pl.pallas_call(
        gather_kernel,
        out_shape=(
            sds((4, 2, 2, EDGE, RANK), BF16),
            sds((4, 4, EDGE, RANK), BF16),
            sds((2, section, RANK), BF16),
        ),
        in_specs=vmem(3),
        out_specs=tuple(vmem(3)),
        scratch_shapes=[pltpu.SemaphoreType.DMA((copies,)), pltpu.SemaphoreType.DMA((copies,))],
        compiler_params=pltpu.CompilerParams(
            collective_id=0, has_side_effects=True, vmem_limit_bytes=48 << 20
        ),
        name="gather",
    )(factor_rows, factor_cols, factor_time)
    smem = pl.BlockSpec(memory_space=pltpu.SMEM)
    sum_a, sum_b, sum_c = pl.pallas_call(
        tile_kernel,
        out_shape=(
            sds((16, EDGE, RANK), F32),
            sds((16, EDGE, RANK), F32),
            sds((section, RANK), F32),
        ),
        in_specs=[smem, smem, pl.BlockSpec(memory_space=pl.ANY)] + vmem(3),
        out_specs=tuple(vmem(3)),
        scratch_shapes=[
            pltpu.VMEM((slots, EDGE, EDGE), BF16),
            pltpu.VMEM((section, RANK), F32),
            pltpu.SemaphoreType.DMA((LOADS,)),
        ],
        compiler_params=pltpu.CompilerParams(vmem_limit_bytes=56 << 20),
        name="tiles",
    )(
        coords,
        count,
        values,
        a_full.reshape(16, EDGE, RANK),
        b_full.reshape(16, EDGE, RANK),
        factor_time,
    )
    wire = lambda *lead: pltpu.VMEM(lead + (RANK,), I16)
    held = lambda *lead: pltpu.VMEM(lead + (RANK,), F32)
    big, small = EDGE + PAD, 32 + PAD
    scratch = dict(
        chip=held(4, 2, EDGE), pair=held(2, EDGE), total_a=held(EDGE), total_b=held(EDGE),
        core_s=wire(4, 2, big), core_r=wire(4, 2, big),
        y_s=wire(6, big), y_r=wire(6, big), x_s=wire(big), x_r=wire(big),
        mid0=held(4, 64), mid1=held(4, 64),
        l1_s=wire(6, big), l1_r=wire(6, big), l2_s=wire(6, small), l2_r=wire(6, small),
        h1_s=wire(6, big), h1_r=wire(6, big), h2_s=wire(6, small), h2_r=wire(6, small),
        gram_a=held(RANK), gram_b=held(RANK),
        ga4=held(4, 16), ga2=held(2, 16), ga=held(4, 2, 2, 16),
        gb4=held(4, 16), gb2=held(2, 16), gb=held(4, 4, 16),
        cy4=held(4, section), cy2=held(2, section), cz4=held(4, section), cz2=held(2, section),
        total_c=held(section),
    )
    copies = 96
    return pl.pallas_call(
        reduce_kernel,
        out_shape=(
            sds((1, EDGE, RANK), F32),
            sds((1, EDGE, RANK), F32),
            sds((section, RANK), F32),
        ),
        in_specs=vmem(6),
        out_specs=tuple(vmem(3)),
        scratch_shapes=[
            scratch,
            pltpu.SemaphoreType.DMA((copies,)),
            pltpu.SemaphoreType.DMA((copies,)),
        ],
        compiler_params=pltpu.CompilerParams(
            collective_id=1, has_side_effects=True, vmem_limit_bytes=56 << 20
        ),
        name="reduce",
    )(
        sum_a.reshape(4, 2, 2, EDGE, RANK),
        sum_b.reshape(4, 4, EDGE, RANK),
        sum_c,
        a_full,
        b_full,
        c_full,
    )


def solution(mesh):
    return jax.shard_map(
        on_device,
        mesh=mesh,
        in_specs=(
            P("row", "col", "tm", None, None, None),
            P("row", "col", "tm", None, None),
            P("row", "col", "tm"),
            P("row", ("col", "tm"), None),
            P("col", ("row", "tm"), None),
            P("tm", None),
        ),
        out_specs=(P("row", ("col", "tm"), None), P("col", ("row", "tm"), None), P("tm", None)),
        check_vma=False,
    )
```

```python
import jax
import jax.numpy as jnp
from jax import lax
from jax.experimental import pallas as pl
from jax.experimental.pallas import tpu as pltpu
from jax.sharding import PartitionSpec as P

F32 = jnp.float32
BF16 = jnp.bfloat16
I16 = jnp.int16
MESH = pl.DeviceIdType.MESH
EDGE = 128
RANK = 256
PAD = 16


class Net:
    def __init__(self, send, recv):
        self.send, self.recv, self.used, self.open = send, recv, 0, []

    def copy(self, src, dst, device):
        made = pltpu.make_async_remote_copy(
            src_ref=src,
            dst_ref=dst,
            send_sem=self.send.at[self.used],
            recv_sem=self.recv.at[self.used],
            device_id=device,
            device_id_type=MESH,
        )
        self.used += 1
        made.start()
        self.open.append(made)
        return made

    def close(self):
        for made in self.open:
            made.wait_send()


class Place:
    def __init__(self):
        row, col, self.t = lax.axis_index("row"), lax.axis_index("col"), lax.axis_index("tm")
        self.z, self.y, self.core = row // 2, col // 2, col % 2
        self.x = (row % 2) * 2 + self.t

    def at(self, dz=0, dy=0, dx=0, other=False):
        z, y, x = (self.z + dz) % 4, (self.y + dy) % 4, (self.x + dx) % 4
        core = 1 - self.core if other else self.core
        return (z * 2 + x // 2, y * 2 + core, x % 2)

    def pair(self):
        return (self.z * 2 + self.x // 2, self.y * 2 + self.core, 1 - self.t)

    def greet(self):
        barrier = pltpu.get_barrier_semaphore()
        others = [self.at(other=True)]
        for step in (1, 2, 3):
            others += [self.at(dz=step), self.at(dy=step), self.at(dx=step)]
        for device in others:
            pl.semaphore_signal(barrier, inc=1, device_id=device, device_id_type=MESH)
        pl.semaphore_wait(barrier, len(others))


def drive(*runs):
    runs = list(runs)
    while runs:
        for run in list(runs):
            if next(run, None) is None:
                runs.remove(run)


def spread(net, view, me, devices):
    made = [net.copy(view(me), view(me), device) for device in devices]
    yield 1
    for copy in made:
        copy.wait_recv()


def swap(net, src, dst, device):
    made = net.copy(src, dst, device)
    yield 1
    made.wait_recv()


def encode(wire, value):
    rows = value.shape[0]
    top = jnp.max(jnp.abs(value), axis=0, keepdims=True)
    power = jnp.ceil(jnp.log2(jnp.maximum(top, 1e-30)))
    coded = jnp.clip(value * jnp.exp2(15.0 - power), -32767.0, 32767.0)
    wire[0:rows] = jnp.round(coded).astype(jnp.int32).astype(I16)
    power = jnp.broadcast_to(power, (PAD, value.shape[1]))
    wire[rows : rows + PAD] = power.astype(jnp.int32).astype(I16)


def decode(wire):
    rows = wire.shape[0] - PAD
    power = wire[rows : rows + PAD].astype(jnp.int32).astype(F32)[0:1]
    return wire[0:rows].astype(jnp.int32).astype(F32) * jnp.exp2(power - 15.0)


SLOTS = 384
ROUND = 2
PADDED = SLOTS + 16 * (ROUND - 1)
ROUNDS = PADDED // ROUND
LANES = 512
UNROLL = 40
LOADS = 12


def iota(shape, dim):
    return lax.broadcasted_iota(jnp.int32, shape, dim)


def up_to_round(n):
    return (n + (ROUND - 1)) // ROUND * ROUND


def lane_sum(value):
    return jnp.sum(value.astype(F32), axis=1, keepdims=True).astype(jnp.int32)


def plan_groups(plan, line, key_row, key_col, entry):
    lane = iota((1, 128), 1)
    count = jnp.sum((key_col == lane).astype(jnp.int32), axis=0, keepdims=True)
    padded = up_to_round(count)
    group = iota((16, 128), 0)
    held = jnp.zeros((16, 128), jnp.int32)
    for m in range(SLOTS // 128):
        held += (key_row[:, 128 * m : 128 * m + 128] == group).astype(jnp.int32)
    tall = up_to_round(lane_sum(held))
    end = jnp.sum(jnp.where(group <= iota((16, 128), 1), tall, 0), axis=0, keepdims=True)
    plan[line + 1 : line + 2, 0:128] = jnp.clip((end - padded) // ROUND, 0, ROUNDS)
    plan[line + 2 : line + 3, 0:128] = jnp.clip(end // ROUND, 0, ROUNDS)
    found = [jnp.zeros((1, 128), jnp.int32) for _ in range(LANES // 128)]
    for c in range(SLOTS // 128):
        mine = key_col[128 * c : 128 * c + 128]
        before = jnp.where(iota((128, 128), 1) < mine, padded, 0)
        for m in range(SLOTS // 128):
            same = key_row[:, 128 * m : 128 * m + 128] == mine
            earlier = iota((128, 128), 1) + 128 * m < iota((128, 128), 0) + 128 * c
            before += (same & earlier).astype(jnp.int32)
        place = lane_sum(before)
        told = entry[128 * c : 128 * c + 128]
        for q in range(LANES // 128):
            hit = place == iota((128, 128), 1) + 128 * q
            found[q] += jnp.sum(jnp.where(hit, told, 0), axis=0, keepdims=True)
    for q in range(LANES // 128):
        plan[line : line + 1, 128 * q : 128 * q + 128] = found[q]


def make_plan(plan, coords, live):
    rows, cols, snaps = coords[0], coords[1], coords[2]
    slot = iota((1, SLOTS), 1)
    row = jnp.where(slot < live, snaps + 32, 0)
    entry = slot + rows * 512 + cols * 8192 + row * 131072
    tall = jnp.concatenate(
        [jnp.broadcast_to(entry[:, 128 * c : 128 * c + 128], (128, 128)).T for c in range(3)],
        axis=0,
    )
    plan_groups(plan, 0, rows, (tall >> 9) & 15, tall)
    plan_groups(plan, 3, cols, (tall >> 13) & 15, tall)


def gather_rows(net, at, full):
    own = full.at[at.y, at.core, at.t]
    pair = net.copy(own, own, at.pair())
    mine = [net.copy(own, own, at.at(dy=k)) for k in (1, 3, 2)]
    yield 1
    pair.wait_recv()
    other = full.at[at.y, at.core, 1 - at.t]
    far = [net.copy(other, other, at.at(dy=k)) for k in (1, 3, 2)]
    near = full.at[at.y, at.core]
    across = [net.copy(near, near, at.at(other=True))]
    yield 1
    for k, first, second in zip((1, 3, 2), mine, far):
        first.wait_recv()
        second.wait_recv()
        came = full.at[(at.y + 4 - k) % 4, at.core]
        across.append(net.copy(came, came, at.at(other=True)))
    yield 1
    for copy in across:
        copy.wait_recv()


def gather_cols(net, at, full):
    def low(z):
        return full.at[z, at.x, 0:64]

    def high(x):
        return full.at[at.z, x, 64:128]

    order = (1, 3, 2)
    low_in = [net.copy(low(at.z), low(at.z), at.at(dz=k)) for k in order]
    high_in = [net.copy(high(at.x), high(at.x), at.at(dx=k)) for k in order]
    rest = []
    for k in order:
        rest.append(net.copy(low(at.z), low(at.z), at.at(dx=k)))
        rest.append(net.copy(high(at.x), high(at.x), at.at(dz=k)))
    yield 1
    for k, from_z, from_x in zip(order, low_in, high_in):
        from_z.wait_recv()
        came = low((at.z + 4 - k) % 4)
        rest += [net.copy(came, came, at.at(dx=j)) for j in order]
        from_x.wait_recv()
        came = high((at.x + 4 - k) % 4)
        rest += [net.copy(came, came, at.at(dz=j)) for j in order]
    yield 1
    for copy in rest:
        copy.wait_recv()


def tile_pass(plan, line, trips, held, times, operand, turned, prefix, other=None, dots=None):
    key = 13 if line == 0 else 9
    back = 9 if line == 0 else 13

    @pl.loop(*trips)
    def _(trip):
        total = prefix[trip * (UNROLL // ROUND)]
        for j in range(UNROLL // ROUND):
            for u in range(ROUND):
                place = trip * UNROLL + j * ROUND + u
                entry = plan[line, place]
                tile = held[jnp.minimum(entry & 511, SLOTS - 1)]
                dims = (((0,), (0,)), ((), ())) if turned else (((1,), (0,)), ((), ()))
                prod = lax.dot_general(
                    tile, operand[(entry >> key) & 15], dims, preferred_element_type=F32
                )
                total = total + prod * times[pl.ds((entry >> 17) & 63, 1), :]
                if dots is not None:
                    facing = other[(entry >> back) & 15].astype(F32)
                    dots[pl.ds(place, 1), :] = jnp.sum(facing * prod, axis=0, keepdims=True)
            prefix[trip * (UNROLL // ROUND) + j + 1] = total


def reduce_rows(net, at, block, chip, total, s):
    order = (2, 1, 3, 0)
    made = {}
    for k in order:
        y = (at.y + k) % 4
        for h in range(2):
            encode(s["core_s"].at[k, h], block(y, 1 - at.core, h))
        made[k] = net.copy(s["core_s"].at[k], s["core_r"].at[k], at.at(other=True))
    for k in order:
        y = (at.y + k) % 4
        for h in range(2):
            chip[k, h] = block(y, at.core, h)
    yield 1
    sent = {}
    for k in order:
        made[k].wait_recv()
        for h in range(2):
            value = chip[k, h] + decode(s["core_r"].at[k, h])
            if k:
                encode(s["y_s"].at[k, h], value)
            else:
                chip[0, h] = value
        if k:
            sent[k] = net.copy(s["y_s"].at[k], s["y_r"].at[k], at.at(dy=k))
    yield 1
    for k in (1, 3, 2):
        sent[k].wait_recv()
        for h in range(2):
            chip[0, h] += decode(s["y_r"].at[k, h])
    encode(s["x_s"], chip[0, 1 - at.t])
    yield from swap(net, s["x_s"], s["x_r"], at.pair())
    total[...] = chip[0, at.t] + decode(s["x_r"])


def reduce_cols(net, at, block, first, second, here, total, s1, r1, s2, r2):
    order = (2, 1, 3, 0)
    made = {}
    for k in order:
        for j in (2, 1, 3):
            encode(s1.at[k, j], block(k, j))
            made[k, j] = net.copy(s1.at[k, j], r1.at[k, j], at.at(**{first: j}))
        yield 1
    sent = {}
    for k in order:
        for j in (1, 3, 2):
            made[k, j].wait_recv()
        value = block(k, 0)
        for j in (1, 3, 2):
            value = value + decode(r1.at[k, j])
        if k:
            encode(s2.at[k], value)
            sent[k] = net.copy(s2.at[k], r2.at[k], at.at(**{second: k}))
        else:
            here[...] = value
        yield 1
    value = here[...]
    for k in (2, 1, 3):
        sent[k].wait_recv()
        value = value + decode(r2.at[k])
    total(value)


def along(at, name):
    return [at.at(**{name: step}) for step in (1, 2, 3)]


def sum_four(ref):
    return (ref[0] + ref[1]) + (ref[2] + ref[3])


def gram_rows(net, at, whole, four, two, full):
    block = (at.y * 4 + at.core * 2 + at.t) * 16
    four[at.z] = whole[pl.ds(pl.multiple_of(block, 16), 16), :]
    yield from spread(net, lambda p: four.at[p], at.z, along(at, "dz"))
    two[0] = sum_four(four)
    yield from swap(net, two.at[0], two.at[1], at.at(dx=2))
    full[at.y, at.core, at.t] = two[0] + two[1]
    yield from swap(net, full.at[at.y, at.core, at.t], full.at[at.y, at.core, at.t], at.pair())
    yield from spread(net, lambda p: full.at[p, at.core], at.y, along(at, "dy"))
    yield from swap(net, full.at[:, at.core], full.at[:, at.core], at.at(other=True))


def gram_cols(net, at, whole, four, two, full):
    block = (at.z * 4 + at.x) * 16
    four[at.y] = whole[pl.ds(pl.multiple_of(block, 16), 16), :]
    yield from spread(net, lambda p: four.at[p], at.y, along(at, "dy"))
    two[0] = sum_four(four)
    yield from swap(net, two.at[0], two.at[1], at.at(other=True))
    full[at.z, at.x] = two[0] + two[1]
    yield from spread(net, lambda p: full.at[p, at.x], at.z, along(at, "dz"))
    yield from spread(net, lambda p: full.at[:, p], at.x, along(at, "dx"))


def reduce_time(net, at, part, four_y, two_y, four_z, two_z, total):
    four_y[at.y] = part[...]
    yield from spread(net, lambda p: four_y.at[p], at.y, along(at, "dy"))
    two_y[0] = sum_four(four_y)
    yield from swap(net, two_y.at[0], two_y.at[1], at.at(other=True))
    four_z[at.z] = two_y[0] + two_y[1]
    yield from spread(net, lambda p: four_z.at[p], at.z, along(at, "dz"))
    two_z[0] = sum_four(four_z)
    yield from swap(net, two_z.at[0], two_z.at[1], at.at(dx=2))
    total[...] = two_z[0] + two_z[1]


def exact_dot(left, right):
    high = right.astype(BF16)
    rest = right - high.astype(F32)
    mid = rest.astype(BF16)
    low = (rest - mid.astype(F32)).astype(BF16)
    return (
        jnp.dot(left, low, preferred_element_type=F32)
        + jnp.dot(left, mid, preferred_element_type=F32)
        + jnp.dot(left, high, preferred_element_type=F32)
    )


def gram(ref):
    block = ref[...]
    return lax.dot_general(block, block, (((0,), (0,)), ((), ())), preferred_element_type=F32)


def gradient_kernel(
    coords, count, values, rows, cols, times, grad_a, grad_b, grad_c, s, plan, send, recv, local
):
    at = Place()
    net = Net(send, recv)
    a_full, b_full, c_full = s["a"], s["b"], s["c"]
    a_flat = a_full.reshape(16, EDGE, RANK)
    b_flat = b_full.reshape(16, EDGE, RANK)
    held, prefix = s["held"], s["prefix"]
    own = [
        pltpu.make_async_copy(cols.at[0], b_full.at[at.z, at.x], local.at[0]),
        pltpu.make_async_copy(rows.at[0], a_full.at[at.y, at.core, at.t], local.at[1]),
        pltpu.make_async_copy(times, c_full.at[at.t], local.at[2]),
        pltpu.make_async_copy(coords, s["coords"], local.at[3]),
    ]
    for copy in own:
        copy.start()
    part = SLOTS // LOADS
    loads = [
        pltpu.make_async_copy(
            values.at[part * i : part * i + part], held.at[part * i : part * i + part], local.at[4 + i]
        )
        for i in range(LOADS)
    ]
    for copy in loads:
        copy.start()
    at.greet()
    for copy in own:
        copy.wait()
    bring_b = gather_cols(net, at, b_full)
    bring_a = gather_rows(net, at, a_full)
    bring_c = swap(net, c_full.at[at.t], c_full.at[at.t], at.pair())
    next(bring_b)
    next(bring_a)
    next(bring_c)

    s["times"][0:32] = jnp.zeros((32, RANK), F32)
    s["times"][32:64] = c_full[at.t].astype(F32)
    prefix[0] = jnp.zeros((EDGE, RANK), F32)
    s["dots"][PADDED:LANES] = jnp.zeros((LANES - PADDED, RANK), F32)
    s["plan"][6:8] = jnp.zeros((2, LANES), jnp.int32)
    s["plan"][1:3] = jnp.zeros((2, LANES), jnp.int32)
    s["plan"][4:6] = jnp.zeros((2, LANES), jnp.int32)
    make_plan(s["plan"], s["coords"], count[0])
    tell = pltpu.make_async_copy(s["plan"], plan, local.at[4 + LOADS])
    tell.start()
    next(bring_b)
    next(bring_a)
    tell.wait()
    for copy in loads:
        copy.wait()
    drive(bring_b, bring_c)

    s["gram"][...] = gram(s["b"].reshape(16 * EDGE, RANK))
    share_b = gram_cols(net, at, s["gram"], s["gb4"], s["gb2"], s["gb"])
    next(share_b)
    next(bring_a)
    trips = PADDED // UNROLL
    tile_pass(plan, 0, (0, trips), held, s["times"], b_flat, False, prefix)

    def row_block(y, core, t):
        i = y * 4 + core * 2 + t
        return prefix[plan[2, i]] - prefix[plan[1, i]]

    part_a = reduce_rows(net, at, row_block, s["chip"], s["total_a"], s)
    next(part_a)
    drive(bring_a)
    next(share_b)
    s["gram"][...] = gram(s["a"].reshape(16 * EDGE, RANK))
    share_a = gram_rows(net, at, s["gram"], s["ga4"], s["ga2"], s["ga"])
    next(share_a)

    def more(first, last):
        tile_pass(
            plan, 3, (first, last), held, s["times"], a_flat, True, prefix, b_flat, s["dots"]
        )

    more(0, 5)
    next(part_a)
    next(share_b)
    next(share_a)
    more(5, trips)

    def col_block(z, x, h):
        i = z * 4 + x
        lanes = slice(128 * h, 128 * h + 128)
        return prefix[plan[5, i], :, lanes] - prefix[plan[4, i], :, lanes]

    def put(h):
        def total(value):
            s["total_b"][:, 128 * h : 128 * h + 128] = value

        return total

    part_b = [
        reduce_cols(
            net, at, lambda k, j: col_block((at.z + k) % 4, (at.x + j) % 4, 0),
            "dx", "dz", s["here0"], put(0), s["s10"], s["r10"], s["s20"], s["r20"],
        ),
        reduce_cols(
            net, at, lambda k, j: col_block((at.z + j) % 4, (at.x + k) % 4, 1),
            "dz", "dx", s["here1"], put(1), s["s11"], s["r11"], s["s21"], s["r21"],
        ),
    ]
    for run in part_b:
        next(run)
    snaps = s["plan"][3:4] >> 17
    pick = (snaps == iota((32, LANES), 0) + 32).astype(F32).astype(BF16)
    s["part_c"][...] = exact_dot(pick, s["dots"][...])
    part_c = reduce_time(
        net, at, s["part_c"], s["cy4"], s["cy2"], s["cz4"], s["cz2"], s["total_c"]
    )
    next(part_c)
    for _ in range(3):
        for run in part_b:
            next(run)
    drive(part_a, share_a, share_b, part_c, *part_b)

    whole_a = s["ga"][...].reshape(RANK, RANK)
    whole_b = s["gb"][...].reshape(RANK, RANK)
    whole_c = gram(c_full.reshape(64, RANK))
    grad_a[0] = exact_dot(a_full[at.y, at.core, at.t], whole_b * whole_c) - s["total_a"][...]
    grad_b[0] = exact_dot(b_full[at.z, at.x], whole_a * whole_c) - s["total_b"][...]
    grad_c[...] = exact_dot(c_full[at.t], whole_a * whole_b) - s["total_c"][...]
    net.close()


def hand_over(in_a, in_b, in_c, out_a, out_b, out_c, sems):
    made = [
        pltpu.make_async_copy(src, dst, sems.at[i])
        for i, (src, dst) in enumerate(((in_a, out_a), (in_b, out_b), (in_c, out_c)))
    ]
    for copy in made:
        copy.start()
    for copy in made:
        copy.wait()


def on_device(tile_values, tile_coords, tile_counts, factor_rows, factor_cols, factor_time):
    values = tile_values.reshape(SLOTS, EDGE, EDGE)
    coords = tile_coords.reshape(3, 1, SLOTS)
    count = tile_counts.reshape(1)
    wire = lambda *lead: pltpu.VMEM(lead + (RANK,), I16)
    half = lambda *lead: pltpu.VMEM(lead + (EDGE,), I16)
    real = lambda *lead: pltpu.VMEM(lead + (RANK,), F32)
    big = EDGE + PAD
    scratch = dict(
        a=pltpu.VMEM((4, 2, 2, EDGE, RANK), BF16),
        b=pltpu.VMEM((4, 4, EDGE, RANK), BF16),
        c=pltpu.VMEM((2, 32, RANK), BF16),
        held=pltpu.VMEM((SLOTS, EDGE, EDGE), BF16),
        prefix=real(ROUNDS + 1, EDGE),
        dots=real(LANES), times=real(64), part_c=real(32),
        plan=pltpu.VMEM((8, LANES), jnp.int32), coords=pltpu.VMEM((3, 1, SLOTS), jnp.int32),
        chip=real(4, 2, EDGE), total_a=real(EDGE), total_b=real(EDGE), total_c=real(32),
        core_s=wire(4, 2, big), core_r=wire(4, 2, big),
        y_s=wire(4, 2, big), y_r=wire(4, 2, big), x_s=wire(big), x_r=wire(big),
        s10=half(4, 4, big), r10=half(4, 4, big), s20=half(4, big), r20=half(4, big),
        s11=half(4, 4, big), r11=half(4, 4, big), s21=half(4, big), r21=half(4, big),
        here0=pltpu.VMEM((EDGE, EDGE), F32), here1=pltpu.VMEM((EDGE, EDGE), F32),
        gram=real(RANK),
        ga4=real(4, 16), ga2=real(2, 16), ga=real(4, 2, 2, 16),
        gb4=real(4, 16), gb2=real(2, 16), gb=real(4, 4, 16),
        cy4=real(4, 32), cy2=real(2, 32), cz4=real(4, 32), cz2=real(2, 32),
    )
    smem = pl.BlockSpec(memory_space=pltpu.SMEM)
    anywhere = pl.BlockSpec(memory_space=pl.ANY)
    whole = pl.BlockSpec(memory_space=pltpu.VMEM)
    shapes = (
        jax.ShapeDtypeStruct((1, EDGE, RANK), F32),
        jax.ShapeDtypeStruct((1, EDGE, RANK), F32),
        jax.ShapeDtypeStruct((32, RANK), F32),
    )
    copies = 128
    grads = pl.pallas_call(
        gradient_kernel,
        out_shape=shapes,
        in_specs=[anywhere, smem] + [anywhere] * 4,
        out_specs=(whole,) * 3,
        scratch_shapes=[
            scratch,
            pltpu.SMEM((8, LANES), jnp.int32),
            pltpu.SemaphoreType.DMA((copies,)),
            pltpu.SemaphoreType.DMA((copies,)),
            pltpu.SemaphoreType.DMA((5 + LOADS,)),
        ],
        compiler_params=pltpu.CompilerParams(
            collective_id=0, has_side_effects=True, vmem_limit_bytes=60 << 20
        ),
        name="gradient",
    )(coords, count, values, factor_rows, factor_cols, factor_time)
    return pl.pallas_call(
        hand_over,
        out_shape=shapes,
        in_specs=[anywhere] * 3,
        out_specs=(anywhere,) * 3,
        scratch_shapes=[pltpu.SemaphoreType.DMA((3,))],
        name="hand_over",
    )(*grads)


def solution(mesh):
    return jax.shard_map(
        on_device,
        mesh=mesh,
        in_specs=(
            P("row", "col", "tm", None, None, None),
            P("row", "col", "tm", None, None),
            P("row", "col", "tm"),
            P("row", ("col", "tm"), None),
            P("col", ("row", "tm"), None),
            P("tm", None),
        ),
        out_specs=(P("row", ("col", "tm"), None), P("col", ("row", "tm"), None), P("tm", None)),
        check_vma=False,
    )
```

```python
from types import FunctionType

import jax
import jax.numpy as jnp
from jax import lax
from jax.experimental import pallas as pl
from jax.experimental.pallas import tpu as pltpu
from jax.sharding import PartitionSpec as P

F32 = jnp.float32
BF16 = jnp.bfloat16
I16 = jnp.int16
MESH = pl.DeviceIdType.MESH
EDGE = 128
RANK = 256
PAD = 16


class Copy:
    def __init__(self, src, dst, send, recv, device):
        self.src, self.dst, self.send, self.recv, self.device = src, dst, send, recv, device

    def made(self):
        return pltpu.make_async_remote_copy(
            src_ref=self.src() if isinstance(self.src, FunctionType) else self.src,
            dst_ref=self.dst() if isinstance(self.dst, FunctionType) else self.dst,
            send_sem=self.send(),
            recv_sem=self.recv(),
            device_id=self.device,
            device_id_type=MESH,
        )

    def wait_recv(self):
        self.made().wait_recv()

    def wait_send(self):
        self.made().wait_send()


class Net:
    def __init__(self, send, recv):
        self.send, self.recv, self.used, self.open = send, recv, 0, []

    def copy(self, src, dst, device):
        n = self.used
        copy = Copy(src, dst, lambda: self.send.at[n], lambda: self.recv.at[n], device)
        self.used += 1
        copy.made().start()
        self.open.append(copy)
        return copy

    def close(self):
        for copy in self.open:
            copy.wait_send()


class Place:
    def __init__(self):
        row, col, self.t = lax.axis_index("row"), lax.axis_index("col"), lax.axis_index("tm")
        self.z, self.y, self.core = row // 2, col // 2, col % 2
        self.x = (row % 2) * 2 + self.t
        self.far_t, self.far_core = 1 - self.t, 1 - self.core
        self.zs = [self.z] + [(self.z + k) % 4 for k in (1, 2, 3)]
        self.ys = [self.y] + [(self.y + k) % 4 for k in (1, 2, 3)]
        self.xs = [self.x] + [(self.x + k) % 4 for k in (1, 2, 3)]
        mine = (row, col, self.t)
        self.dz = [mine] + [(z * 2 + self.x // 2, col, self.t) for z in self.zs[1:]]
        self.dy = [mine] + [(row, y * 2 + self.core, self.t) for y in self.ys[1:]]
        self.dx = [mine] + [(self.z * 2 + x // 2, col, x % 2) for x in self.xs[1:]]
        self.other = (row, self.y * 2 + self.far_core, self.t)
        self.pair = (row, col, self.far_t)

    def greet(self):
        barrier = pltpu.get_barrier_semaphore()
        others = [self.other] + self.dz[1:] + self.dy[1:] + self.dx[1:]
        for device in others:
            pl.semaphore_signal(barrier, inc=1, device_id=device, device_id_type=MESH)
        pl.semaphore_wait(barrier, len(others))


def step(run, *more):
    for each in (run,) + more:
        next(each, None)


def drive(*runs):
    runs = list(runs)
    while runs:
        for run in list(runs):
            if next(run, None) is None:
                runs.remove(run)


def spread(net, view, me, devices):
    made = [net.copy(lambda: view(me), lambda: view(me), device) for device in devices]
    yield 1
    for copy in made:
        copy.wait_recv()


def swap(net, src, dst, device):
    made = net.copy(src, dst, device)
    yield 1
    made.wait_recv()


def encode(wire, value):
    rows = value.shape[0]
    top = jnp.max(jnp.abs(value), axis=0, keepdims=True)
    power = jnp.ceil(jnp.log2(jnp.maximum(top, 1e-30)))
    coded = jnp.clip(value * jnp.exp2(15.0 - power), -32767.0, 32767.0)
    wire[0:rows] = jnp.round(coded).astype(jnp.int32).astype(I16)
    power = jnp.broadcast_to(power, (PAD, value.shape[1]))
    wire[rows : rows + PAD] = power.astype(jnp.int32).astype(I16)


def decode(wire):
    rows = wire.shape[0] - PAD
    power = wire[rows : rows + PAD].astype(jnp.int32).astype(F32)[0:1]
    return wire[0:rows].astype(jnp.int32).astype(F32) * jnp.exp2(power - 15.0)


SLOTS = 384
ROUND = 2
PADDED = SLOTS + 16 * (ROUND - 1)
ROUNDS = PADDED // ROUND
LANES = 512
UNROLL = 40
LOADS = 12


def iota(shape, dim):
    return lax.broadcasted_iota(jnp.int32, shape, dim)


def up_to_round(n):
    return (n + (ROUND - 1)) // ROUND * ROUND


def lane_sum(value):
    return jnp.sum(value.astype(F32), axis=1, keepdims=True).astype(jnp.int32)


def plan_groups(plan, line, key_row, key_col, entry):
    lane = iota((1, 128), 1)
    count = jnp.sum((key_col == lane).astype(jnp.int32), axis=0, keepdims=True)
    padded = up_to_round(count)
    group = iota((16, 128), 0)
    held = jnp.zeros((16, 128), jnp.int32)
    for m in range(SLOTS // 128):
        held += (key_row[:, 128 * m : 128 * m + 128] == group).astype(jnp.int32)
    tall = up_to_round(lane_sum(held))
    end = jnp.sum(jnp.where(group <= iota((16, 128), 1), tall, 0), axis=0, keepdims=True)
    plan[line + 1 : line + 2, 0:128] = jnp.clip((end - padded) // ROUND, 0, ROUNDS)
    plan[line + 2 : line + 3, 0:128] = jnp.clip(end // ROUND, 0, ROUNDS)
    found = [jnp.zeros((1, 128), jnp.int32) for _ in range(LANES // 128)]
    for c in range(SLOTS // 128):
        mine = key_col[128 * c : 128 * c + 128]
        before = jnp.where(iota((128, 128), 1) < mine, padded, 0)
        for m in range(SLOTS // 128):
            same = key_row[:, 128 * m : 128 * m + 128] == mine
            earlier = iota((128, 128), 1) + 128 * m < iota((128, 128), 0) + 128 * c
            before += (same & earlier).astype(jnp.int32)
        place = lane_sum(before)
        told = entry[128 * c : 128 * c + 128]
        for q in range(LANES // 128):
            hit = place == iota((128, 128), 1) + 128 * q
            found[q] += jnp.sum(jnp.where(hit, told, 0), axis=0, keepdims=True)
    for q in range(LANES // 128):
        plan[line : line + 1, 128 * q : 128 * q + 128] = found[q]


def make_plan(plan, coords, live):
    rows, cols, snaps = coords[0], coords[1], coords[2]
    slot = iota((1, SLOTS), 1)
    row = jnp.where(slot < live, snaps + 32, 0)
    entry = slot + rows * 512 + cols * 8192 + row * 131072
    tall = jnp.concatenate(
        [jnp.broadcast_to(entry[:, 128 * c : 128 * c + 128], (128, 128)).T for c in range(3)],
        axis=0,
    )
    plan_groups(plan, 0, rows, (tall >> 9) & 15, tall)
    plan_groups(plan, 3, cols, (tall >> 13) & 15, tall)


def gather_rows(net, at, full, source):
    own = full.at[at.y, at.core, at.t]
    pair = net.copy(source, own, at.pair)
    mine = [net.copy(source, own, at.dy[k]) for k in (1, 3, 2)]
    yield 1
    pair.wait_recv()
    other = full.at[at.y, at.core, at.far_t]
    far = [net.copy(other, other, at.dy[k]) for k in (1, 3, 2)]
    near = full.at[at.y, at.core]
    across = [net.copy(near, near, at.other)]
    yield 1
    for k, first, second in zip((1, 3, 2), mine, far):
        first.wait_recv()
        second.wait_recv()
        came = full.at[at.ys[4 - k], at.core]
        across.append(net.copy(came, came, at.other))
    yield 1
    for copy in across:
        copy.wait_recv()


def gather_cols(net, at, full, source):
    def low(z):
        return full.at[z, at.x, 0:64]

    def high(x):
        return full.at[at.z, x, 64:128]

    order = (1, 3, 2)
    own_low, own_high = source.at[0:64], source.at[64:128]
    low_in = [net.copy(own_low, low(at.z), at.dz[k]) for k in order]
    high_in = [net.copy(own_high, high(at.x), at.dx[k]) for k in order]
    rest = []
    for k in order:
        rest.append(net.copy(own_low, low(at.z), at.dx[k]))
        rest.append(net.copy(own_high, high(at.x), at.dz[k]))
    yield 1
    for k, from_z, from_x in zip(order, low_in, high_in):
        from_z.wait_recv()
        came = low(at.zs[4 - k])
        rest += [net.copy(came, came, at.dx[j]) for j in order]
        from_x.wait_recv()
        came = high(at.xs[4 - k])
        rest += [net.copy(came, came, at.dz[j]) for j in order]
    yield 1
    for copy in rest:
        copy.wait_recv()


def tile_pass(plan, line, held, times, operand, turned, prefix, hooks, other=None, dots=None):
    key = 13 if line == 0 else 9
    back = 9 if line == 0 else 13

    @pl.loop(0, PADDED // UNROLL)
    def _(trip):
        for when, hook in hooks.items():
            pl.when(trip == when)(hook)
        total = prefix[trip * (UNROLL // ROUND)]
        for j in range(UNROLL // ROUND):
            for u in range(ROUND):
                place = trip * UNROLL + j * ROUND + u
                entry = plan[line, place]
                tile = held[jnp.minimum(entry & 511, SLOTS - 1)]
                dims = (((0,), (0,)), ((), ())) if turned else (((1,), (0,)), ((), ()))
                prod = lax.dot_general(
                    tile, operand[(entry >> key) & 15], dims, preferred_element_type=F32
                )
                total = total + prod * times[pl.ds((entry >> 17) & 63, 1), :]
                if dots is not None:
                    facing = other[(entry >> back) & 15].astype(F32)
                    dots[pl.ds(place, 1), :] = jnp.sum(facing * prod, axis=0, keepdims=True)
            prefix[trip * (UNROLL // ROUND) + j + 1] = total


def at_step(ref, k):
    return lambda: ref.at[k]


def reduce_rows(net, at, block, chip, total, s):
    order = (2, 1, 3, 0)
    made = {}
    for k in order:
        for h in range(2):
            encode(s["core_s"].at[k, h], block(at.ys[k], at.far_core, h))
        made[k] = net.copy(at_step(s["core_s"], k), at_step(s["core_r"], k), at.other)
    for k in order:
        for h in range(2):
            chip[k, h] = block(at.ys[k], at.core, h)
    yield 1
    sent = {}
    for k in order:
        made[k].wait_recv()
        for h in range(2):
            value = chip[k, h] + decode(s["core_r"].at[k, h])
            if k:
                encode(s["y_s"].at[k, h], value)
            else:
                chip[0, h] = value
        if k:
            sent[k] = net.copy(at_step(s["y_s"], k), at_step(s["y_r"], k), at.dy[k])
    yield 1
    for k in (1, 3, 2):
        sent[k].wait_recv()
        for h in range(2):
            chip[0, h] += decode(s["y_r"].at[k, h])
    encode(s["x_s"], chip[0, at.far_t])
    yield from swap(net, s["x_s"], s["x_r"], at.pair)
    total[...] = chip[0, at.t] + decode(s["x_r"])


def reduce_cols(net, block, first, second, here, total, s1, r1, s2, r2):
    order = (2, 1, 3, 0)
    made = {}
    for k in order:
        for j in (2, 1, 3):
            encode(s1.at[k, j], block(k, j))
            made[k, j] = net.copy(s1.at[k, j], r1.at[k, j], first[j])
        yield 1
    sent = {}
    for k in order:
        for j in (1, 3, 2):
            made[k, j].wait_recv()
        value = block(k, 0)
        for j in (1, 3, 2):
            value = value + decode(r1.at[k, j])
        if k:
            encode(s2.at[k], value)
            sent[k] = net.copy(s2.at[k], r2.at[k], second[k])
        else:
            here[...] = value
        yield 1
    value = here[...]
    for k in (2, 1, 3):
        sent[k].wait_recv()
        value = value + decode(r2.at[k])
    total(value)


def sum_four(ref):
    return (ref[0] + ref[1]) + (ref[2] + ref[3])


def gram_rows(net, at, whole, four, two, full):
    block = (at.y * 4 + at.core * 2 + at.t) * 16
    four[at.z] = whole[pl.ds(pl.multiple_of(block, 16), 16), :]
    yield from spread(net, lambda p: four.at[p], at.z, at.dz[1:])
    two[0] = sum_four(four)
    yield from swap(net, at_step(two, 0), at_step(two, 1), at.dx[2])
    full[at.y, at.core, at.t] = two[0] + two[1]
    yield from swap(net, lambda: full.at[at.y, at.core, at.t], lambda: full.at[at.y, at.core, at.t], at.pair)
    yield from spread(net, lambda p: full.at[p, at.core], at.y, at.dy[1:])
    yield from swap(net, lambda: full.at[:, at.core], lambda: full.at[:, at.core], at.other)


def gram_cols(net, at, whole, four, two, full):
    block = (at.z * 4 + at.x) * 16
    four[at.y] = whole[pl.ds(pl.multiple_of(block, 16), 16), :]
    yield from spread(net, lambda p: four.at[p], at.y, at.dy[1:])
    two[0] = sum_four(four)
    yield from swap(net, at_step(two, 0), at_step(two, 1), at.other)
    full[at.z, at.x] = two[0] + two[1]
    yield from spread(net, lambda p: full.at[p, at.x], at.z, at.dz[1:])
    yield from spread(net, lambda p: full.at[:, p], at.x, at.dx[1:])


def reduce_time(net, at, part, four_y, two_y, four_z, two_z, total):
    four_y[at.y] = part[...]
    yield from spread(net, lambda p: four_y.at[p], at.y, at.dy[1:])
    two_y[0] = sum_four(four_y)
    yield from swap(net, at_step(two_y, 0), at_step(two_y, 1), at.other)
    four_z[at.z] = two_y[0] + two_y[1]
    yield from spread(net, lambda p: four_z.at[p], at.z, at.dz[1:])
    two_z[0] = sum_four(four_z)
    yield from swap(net, at_step(two_z, 0), at_step(two_z, 1), at.dx[2])
    total[...] = two_z[0] + two_z[1]


def exact_dot(left, right):
    high = right.astype(BF16)
    rest = right - high.astype(F32)
    mid = rest.astype(BF16)
    low = (rest - mid.astype(F32)).astype(BF16)
    return (
        jnp.dot(left, low, preferred_element_type=F32)
        + jnp.dot(left, mid, preferred_element_type=F32)
        + jnp.dot(left, high, preferred_element_type=F32)
    )


def gram(ref):
    block = ref[...]
    return lax.dot_general(block, block, (((0,), (0,)), ((), ())), preferred_element_type=F32)


def gradient_kernel(
    coords, count, values, rows, cols, times, grad_a, grad_b, grad_c, s, plan, send, recv, local
):
    at = Place()
    net = Net(send, recv)
    a_full, b_full, c_full = s["a"], s["b"], s["c"]
    a_flat = a_full.reshape(16, EDGE, RANK)
    b_flat = b_full.reshape(16, EDGE, RANK)
    held, prefix = s["held"], s["prefix"]
    own = [
        pltpu.make_async_copy(cols.at[0], b_full.at[at.z, at.x], local.at[0]),
        pltpu.make_async_copy(rows.at[0], a_full.at[at.y, at.core, at.t], local.at[1]),
        pltpu.make_async_copy(times, c_full.at[at.t], local.at[2]),
        pltpu.make_async_copy(coords, s["coords"], local.at[3]),
    ]
    for copy in own:
        copy.start()
    part = SLOTS // LOADS
    loads = [
        pltpu.make_async_copy(
            values.at[part * i : part * i + part], held.at[part * i : part * i + part], local.at[4 + i]
        )
        for i in range(LOADS)
    ]
    for copy in loads:
        copy.start()
    at.greet()
    bring_b = gather_cols(net, at, b_full, cols.at[0])
    bring_a = gather_rows(net, at, a_full, rows.at[0])
    bring_c = swap(net, times, c_full.at[at.t], at.pair)
    step(bring_b, bring_a, bring_c)
    for copy in own:
        copy.wait()

    s["times"][0:32] = jnp.zeros((32, RANK), F32)
    s["times"][32:64] = c_full[at.t].astype(F32)
    prefix[0] = jnp.zeros((EDGE, RANK), F32)
    s["dots"][PADDED:LANES] = jnp.zeros((LANES - PADDED, RANK), F32)
    for line in (1, 4, 6):
        s["plan"][line : line + 2] = jnp.zeros((2, LANES), jnp.int32)
    make_plan(s["plan"], s["coords"], count[0])
    tell = pltpu.make_async_copy(s["plan"], plan, local.at[4 + LOADS])
    tell.start()
    step(bring_b, bring_a)
    tell.wait()
    for copy in loads:
        copy.wait()
    step(bring_a)
    drive(bring_b, bring_a, bring_c)

    s["gram"][...] = gram(b_full.reshape(16 * EDGE, RANK))
    share_b = gram_cols(net, at, s["gram"], s["gb4"], s["gb2"], s["gb"])
    share_a = gram_rows(net, at, s["gram_a"], s["ga4"], s["ga2"], s["ga"])
    step(share_b)

    def start_a():
        s["gram_a"][...] = gram(a_full.reshape(16 * EDGE, RANK))
        step(share_a)

    hooks = {
        2: start_a,
        4: lambda: step(share_b),
        5: lambda: step(share_a),
        7: lambda: step(share_b),
        8: lambda: step(share_a),
    }
    tile_pass(
        plan, 0, held, s["times"], b_flat, False, prefix, hooks, a_flat, s["dots"]
    )

    def row_block(y, core, t):
        i = y * 4 + core * 2 + t
        return prefix[plan[2, i]] - prefix[plan[1, i]]

    part_a = reduce_rows(net, at, row_block, s["chip"], s["total_a"], s)
    step(part_a)
    snaps = s["plan"][0:1] >> 17
    pick = (snaps == iota((32, LANES), 0) + 32).astype(F32).astype(BF16)
    s["part_c"][...] = exact_dot(pick, s["dots"][...])
    part_c = reduce_time(
        net, at, s["part_c"], s["cy4"], s["cy2"], s["cz4"], s["cz2"], s["total_c"]
    )
    step(part_c)
    hooks = {
        1: lambda: step(share_b),
        2: lambda: step(share_a),
        3: lambda: step(part_a, part_c),
        5: lambda: step(share_b, share_a),
        6: lambda: step(part_c),
        8: lambda: step(share_a),
        9: lambda: step(part_c),
    }
    tile_pass(plan, 3, held, s["times"], a_flat, True, prefix, hooks)

    def col_block(z, x, h):
        i = z * 4 + x
        lanes = slice(128 * h, 128 * h + 128)
        return prefix[plan[5, i], :, lanes] - prefix[plan[4, i], :, lanes]

    def put(h):
        def total(value):
            s["total_b"][:, 128 * h : 128 * h + 128] = value

        return total

    part_b = [
        reduce_cols(
            net, lambda k, j: col_block(at.zs[k], at.xs[j], 0),
            at.dx, at.dz, s["here0"], put(0), s["s10"], s["r10"], s["s20"], s["r20"],
        ),
        reduce_cols(
            net, lambda k, j: col_block(at.zs[j], at.xs[k], 1),
            at.dz, at.dx, s["here1"], put(1), s["s11"], s["r11"], s["s21"], s["r21"],
        ),
    ]
    for _ in range(4):
        step(*part_b)
    step(part_a)
    step(*part_b)
    step(part_c)
    whole_a = s["ga"][...].reshape(RANK, RANK)
    whole_b = s["gb"][...].reshape(RANK, RANK)
    whole_c = gram(c_full.reshape(64, RANK))
    grad_c[...] = exact_dot(c_full[at.t], whole_a * whole_b) - s["total_c"][...]
    s["near_a"][...] = exact_dot(a_full[at.y, at.core, at.t], whole_b * whole_c)
    step(*part_b)
    s["near_b"][...] = exact_dot(b_full[at.z, at.x], whole_a * whole_c)
    step(*part_b)
    step(part_a)
    grad_a[0] = s["near_a"][...] - s["total_a"][...]
    drive(*part_b)
    grad_b[0] = s["near_b"][...] - s["total_b"][...]
    net.close()


def hand_over(in_a, in_b, in_c, out_a, out_b, out_c, held_a, held_b, held_c, sems):
    path = ((in_a, held_a, out_a), (in_b, held_b, out_b), (in_c, held_c, out_c))
    bring = [pltpu.make_async_copy(p[0], p[1], sems.at[i]) for i, p in enumerate(path)]
    leave = [pltpu.make_async_copy(p[1], p[2], sems.at[3 + i]) for i, p in enumerate(path)]
    for copy in bring:
        copy.start()
    for came, gone in zip(bring, leave):
        came.wait()
        gone.start()
    for copy in leave:
        copy.wait()


def on_device(tile_values, tile_coords, tile_counts, factor_rows, factor_cols, factor_time):
    values = tile_values.reshape(SLOTS, EDGE, EDGE)
    coords = tile_coords.reshape(3, 1, SLOTS)
    count = tile_counts.reshape(1)
    wire = lambda *lead: pltpu.VMEM(lead + (RANK,), I16)
    half = lambda *lead: pltpu.VMEM(lead + (EDGE,), I16)
    real = lambda *lead: pltpu.VMEM(lead + (RANK,), F32)
    big = EDGE + PAD
    scratch = dict(
        a=pltpu.VMEM((4, 2, 2, EDGE, RANK), BF16),
        b=pltpu.VMEM((4, 4, EDGE, RANK), BF16),
        c=pltpu.VMEM((2, 32, RANK), BF16),
        held=pltpu.VMEM((SLOTS, EDGE, EDGE), BF16),
        prefix=real(ROUNDS + 1, EDGE),
        dots=real(LANES), times=real(64), part_c=real(32),
        plan=pltpu.VMEM((8, LANES), jnp.int32), coords=pltpu.VMEM((3, 1, SLOTS), jnp.int32),
        chip=real(4, 2, EDGE), total_a=real(EDGE), total_b=real(EDGE), total_c=real(32),
        core_s=wire(4, 2, big), core_r=wire(4, 2, big),
        y_s=wire(4, 2, big), y_r=wire(4, 2, big), x_s=wire(big), x_r=wire(big),
        s10=half(4, 4, big), r10=half(4, 4, big), s20=half(4, big), r20=half(4, big),
        s11=half(4, 4, big), r11=half(4, 4, big), s21=half(4, big), r21=half(4, big),
        here0=pltpu.VMEM((EDGE, EDGE), F32), here1=pltpu.VMEM((EDGE, EDGE), F32),
        gram=real(RANK), gram_a=real(RANK), near_a=real(EDGE), near_b=real(EDGE),
        ga4=real(4, 16), ga2=real(2, 16), ga=real(4, 2, 2, 16),
        gb4=real(4, 16), gb2=real(2, 16), gb=real(4, 4, 16),
        cy4=real(4, 32), cy2=real(2, 32), cz4=real(4, 32), cz2=real(2, 32),
    )
    smem = pl.BlockSpec(memory_space=pltpu.SMEM)
    anywhere = pl.BlockSpec(memory_space=pl.ANY)
    whole = pl.BlockSpec(memory_space=pltpu.VMEM)
    shapes = (
        jax.ShapeDtypeStruct((1, EDGE, RANK), F32),
        jax.ShapeDtypeStruct((1, EDGE, RANK), F32),
        jax.ShapeDtypeStruct((32, RANK), F32),
    )
    copies = 128
    grads = pl.pallas_call(
        gradient_kernel,
        out_shape=shapes,
        in_specs=[anywhere, smem] + [anywhere] * 4,
        out_specs=(whole,) * 3,
        scratch_shapes=[
            scratch,
            pltpu.SMEM((8, LANES), jnp.int32),
            pltpu.SemaphoreType.DMA((copies,)),
            pltpu.SemaphoreType.DMA((copies,)),
            pltpu.SemaphoreType.DMA((5 + LOADS,)),
        ],
        compiler_params=pltpu.CompilerParams(
            collective_id=0, has_side_effects=True, vmem_limit_bytes=60 << 20
        ),
        name="gradient",
    )(coords, count, values, factor_rows, factor_cols, factor_time)
    return pl.pallas_call(
        hand_over,
        out_shape=shapes,
        in_specs=[anywhere] * 3,
        out_specs=(anywhere,) * 3,
        scratch_shapes=[pltpu.VMEM(kind.shape, F32) for kind in shapes]
        + [pltpu.SemaphoreType.DMA((6,))],
        compiler_params=pltpu.CompilerParams(vmem_limit_bytes=60 << 20),
        name="hand_over",
    )(*grads)


def solution(mesh):
    return jax.shard_map(
        on_device,
        mesh=mesh,
        in_specs=(
            P("row", "col", "tm", None, None, None),
            P("row", "col", "tm", None, None),
            P("row", "col", "tm"),
            P("row", ("col", "tm"), None),
            P("col", ("row", "tm"), None),
            P("tm", None),
        ),
        out_specs=(P("row", ("col", "tm"), None), P("col", ("row", "tm"), None), P("tm", None)),
        check_vma=False,
    )
```

```python
from types import FunctionType

import jax
import jax.numpy as jnp
from jax import lax
from jax.experimental import pallas as pl
from jax.experimental.pallas import tpu as pltpu
from jax.sharding import PartitionSpec as P

F32 = jnp.float32
BF16 = jnp.bfloat16
I16 = jnp.int16
MESH = pl.DeviceIdType.MESH
EDGE = 128
RANK = 256
PAD = 16


class Copy:
    def __init__(self, src, dst, send, recv, device):
        self.src, self.dst, self.send, self.recv, self.device = src, dst, send, recv, device

    def made(self):
        return pltpu.make_async_remote_copy(
            src_ref=self.src() if isinstance(self.src, FunctionType) else self.src,
            dst_ref=self.dst() if isinstance(self.dst, FunctionType) else self.dst,
            send_sem=self.send(),
            recv_sem=self.recv(),
            device_id=self.device,
            device_id_type=MESH,
        )

    def wait_recv(self):
        self.made().wait_recv()

    def wait_send(self):
        self.made().wait_send()


class Net:
    def __init__(self, send, recv):
        self.send, self.recv, self.used, self.open = send, recv, 0, []

    def copy(self, src, dst, device):
        n = self.used
        copy = Copy(src, dst, lambda: self.send.at[n], lambda: self.recv.at[n], device)
        self.used += 1
        copy.made().start()
        self.open.append(copy)
        return copy

    def close(self):
        for copy in self.open:
            copy.wait_send()


class Place:
    def __init__(self):
        row, col, self.t = lax.axis_index("row"), lax.axis_index("col"), lax.axis_index("tm")
        self.z, self.y, self.core = row // 2, col // 2, col % 2
        self.x = (row % 2) * 2 + self.t
        self.far_t, self.far_core = 1 - self.t, 1 - self.core
        self.zs = [self.z] + [(self.z + k) % 4 for k in (1, 2, 3)]
        self.ys = [self.y] + [(self.y + k) % 4 for k in (1, 2, 3)]
        self.xs = [self.x] + [(self.x + k) % 4 for k in (1, 2, 3)]
        mine = (row, col, self.t)
        self.dz = [mine] + [(z * 2 + self.x // 2, col, self.t) for z in self.zs[1:]]
        self.dy = [mine] + [(row, y * 2 + self.core, self.t) for y in self.ys[1:]]
        self.dx = [mine] + [(self.z * 2 + x // 2, col, x % 2) for x in self.xs[1:]]
        self.other = (row, self.y * 2 + self.far_core, self.t)
        self.pair = (row, col, self.far_t)

    def greet(self):
        barrier = pltpu.get_barrier_semaphore()
        others = [self.other] + self.dz[1:] + self.dy[1:] + self.dx[1:]
        for device in others:
            pl.semaphore_signal(barrier, inc=1, device_id=device, device_id_type=MESH)
        pl.semaphore_wait(barrier, len(others))


def step(run, *more):
    for each in (run,) + more:
        next(each, None)


def drive(*runs):
    runs = list(runs)
    while runs:
        for run in list(runs):
            if next(run, None) is None:
                runs.remove(run)


def spread(net, view, me, devices):
    made = [net.copy(lambda: view(me), lambda: view(me), device) for device in devices]
    yield 1
    for copy in made:
        copy.wait_recv()


def swap(net, src, dst, device):
    made = net.copy(src, dst, device)
    yield 1
    made.wait_recv()


def encode(wire, value):
    rows = value.shape[0]
    top = jnp.max(jnp.abs(value), axis=0, keepdims=True)
    power = jnp.ceil(jnp.log2(jnp.maximum(top, 1e-30)))
    coded = jnp.clip(value * jnp.exp2(15.0 - power), -32767.0, 32767.0)
    wire[0:rows] = jnp.round(coded).astype(jnp.int32).astype(I16)
    power = jnp.broadcast_to(power, (PAD, value.shape[1]))
    wire[rows : rows + PAD] = power.astype(jnp.int32).astype(I16)


def decode(wire):
    rows = wire.shape[0] - PAD
    power = wire[rows : rows + PAD].astype(jnp.int32).astype(F32)[0:1]
    return wire[0:rows].astype(jnp.int32).astype(F32) * jnp.exp2(power - 15.0)


SLOTS = 384
ROUND = 2
PADDED = SLOTS + 16 * (ROUND - 1)
ROUNDS = PADDED // ROUND
LANES = 512
UNROLL = 40
LOADS = 12


def iota(shape, dim):
    return lax.broadcasted_iota(jnp.int32, shape, dim)


def up_to_round(n):
    return (n + (ROUND - 1)) // ROUND * ROUND


def lane_sum(value):
    return jnp.sum(value.astype(F32), axis=1, keepdims=True).astype(jnp.int32)


def plan_groups(plan, line, key_row, key_col, entry):
    lane = iota((1, 128), 1)
    count = jnp.sum((key_col == lane).astype(jnp.int32), axis=0, keepdims=True)
    padded = up_to_round(count)
    group = iota((16, 128), 0)
    held = jnp.zeros((16, 128), jnp.int32)
    for m in range(SLOTS // 128):
        held += (key_row[:, 128 * m : 128 * m + 128] == group).astype(jnp.int32)
    tall = up_to_round(lane_sum(held))
    end = jnp.sum(jnp.where(group <= iota((16, 128), 1), tall, 0), axis=0, keepdims=True)
    plan[line + 1 : line + 2, 0:128] = jnp.clip((end - padded) // ROUND, 0, ROUNDS)
    plan[line + 2 : line + 3, 0:128] = jnp.clip(end // ROUND, 0, ROUNDS)
    found = [jnp.zeros((1, 128), jnp.int32) for _ in range(LANES // 128)]
    for c in range(SLOTS // 128):
        mine = key_col[128 * c : 128 * c + 128]
        before = jnp.where(iota((128, 128), 1) < mine, padded, 0)
        for m in range(SLOTS // 128):
            same = key_row[:, 128 * m : 128 * m + 128] == mine
            earlier = iota((128, 128), 1) + 128 * m < iota((128, 128), 0) + 128 * c
            before += (same & earlier).astype(jnp.int32)
        place = lane_sum(before)
        told = entry[128 * c : 128 * c + 128]
        for q in range(LANES // 128):
            hit = place == iota((128, 128), 1) + 128 * q
            found[q] += jnp.sum(jnp.where(hit, told, 0), axis=0, keepdims=True)
    for q in range(LANES // 128):
        plan[line : line + 1, 128 * q : 128 * q + 128] = found[q]


def make_plan(plan, coords, live):
    rows, cols, snaps = coords[0], coords[1], coords[2]
    slot = iota((1, SLOTS), 1)
    row = jnp.where(slot < live, snaps + 32, 0)
    entry = slot + rows * 512 + cols * 8192 + row * 131072
    tall = jnp.concatenate(
        [jnp.broadcast_to(entry[:, 128 * c : 128 * c + 128], (128, 128)).T for c in range(3)],
        axis=0,
    )
    plan_groups(plan, 0, rows, (tall >> 9) & 15, tall)
    plan_groups(plan, 3, cols, (tall >> 13) & 15, tall)


def gather_rows(net, at, full, source):
    own = full.at[at.y, at.core, at.t]
    pair = net.copy(source, own, at.pair)
    mine = {k: net.copy(source, own, at.dy[k]) for k in (2, 1, 3)}
    yield 1
    pair.wait_recv()
    other = full.at[at.y, at.core, at.far_t]
    far = {k: net.copy(other, other, at.dy[k]) for k in (2, 1, 3)}
    near = full.at[at.y, at.core]
    across = [net.copy(near, near, at.other)]
    yield 1
    for k in (1, 3, 2):
        mine[k].wait_recv()
        far[k].wait_recv()
        came = full.at[at.ys[4 - k], at.core]
        across.append(net.copy(came, came, at.other))
    yield 1
    for copy in across:
        copy.wait_recv()


def gather_cols(net, at, full, source):
    def low(z):
        return full.at[z, at.x, 0:64]

    def high(x):
        return full.at[at.z, x, 64:128]

    order = (2, 1, 3)
    own_low, own_high = source.at[0:64], source.at[64:128]
    low_in, high_in, rest = {}, {}, []
    for k in order:
        low_in[k] = net.copy(own_low, low(at.z), at.dz[k])
        high_in[k] = net.copy(own_high, high(at.x), at.dx[k])
    for k in order:
        rest.append(net.copy(own_low, low(at.z), at.dx[k]))
        rest.append(net.copy(own_high, high(at.x), at.dz[k]))
    yield 1
    for k in (1, 3, 2):
        low_in[k].wait_recv()
        came = low(at.zs[4 - k])
        rest += [net.copy(came, came, at.dx[j]) for j in order]
        high_in[k].wait_recv()
        came = high(at.xs[4 - k])
        rest += [net.copy(came, came, at.dz[j]) for j in order]
    yield 1
    for copy in rest:
        copy.wait_recv()


def tile_pass(plan, line, held, times, operand, turned, prefix, hooks, other=None, dots=None):
    key = 13 if line == 0 else 9
    back = 9 if line == 0 else 13

    @pl.loop(0, PADDED // UNROLL)
    def _(trip):
        for when, hook in hooks.items():
            pl.when(trip == when)(hook)
        total = prefix[trip * (UNROLL // ROUND)]
        for j in range(UNROLL // ROUND):
            for u in range(ROUND):
                place = trip * UNROLL + j * ROUND + u
                entry = plan[line, place]
                tile = held[jnp.minimum(entry & 511, SLOTS - 1)]
                dims = (((0,), (0,)), ((), ())) if turned else (((1,), (0,)), ((), ()))
                prod = lax.dot_general(
                    tile, operand[(entry >> key) & 15], dims, preferred_element_type=F32
                )
                total = total + prod * times[pl.ds((entry >> 17) & 63, 1), :]
                if dots is not None:
                    facing = other[(entry >> back) & 15].astype(F32)
                    dots[pl.ds(place, 1), :] = jnp.sum(facing * prod, axis=0, keepdims=True)
            prefix[trip * (UNROLL // ROUND) + j + 1] = total


def at_step(ref, k):
    return lambda: ref.at[k]


def reduce_rows(net, at, block, chip, total, s):
    order = (2, 1, 3, 0)
    made = {}
    for k in order:
        for h in range(2):
            encode(s["core_s"].at[k, h], block(at.ys[k], at.far_core, h))
        made[k] = net.copy(at_step(s["core_s"], k), at_step(s["core_r"], k), at.other)
    for k in order:
        for h in range(2):
            chip[k, h] = block(at.ys[k], at.core, h)
    yield 1
    sent = {}
    for k in order:
        made[k].wait_recv()
        for h in range(2):
            value = chip[k, h] + decode(s["core_r"].at[k, h])
            if k:
                encode(s["y_s"].at[k, h], value)
            else:
                chip[0, h] = value
        if k:
            sent[k] = net.copy(at_step(s["y_s"], k), at_step(s["y_r"], k), at.dy[k])
    yield 1
    for k in (1, 3, 2):
        sent[k].wait_recv()
        for h in range(2):
            chip[0, h] += decode(s["y_r"].at[k, h])
    encode(s["x_s"], chip[0, at.far_t])
    yield from swap(net, s["x_s"], s["x_r"], at.pair)
    total[...] = chip[0, at.t] + decode(s["x_r"])


def reduce_cols(net, block, first, second, here, total, s1, r1, s2, r2):
    order = (2, 1, 3, 0)
    made = {}
    for k in order:
        for j in (2, 1, 3):
            encode(s1.at[k, j], block(k, j))
            made[k, j] = net.copy(s1.at[k, j], r1.at[k, j], first[j])
        yield 1
    sent = {}
    for k in order:
        for j in (1, 3, 2):
            made[k, j].wait_recv()
        value = block(k, 0)
        for j in (1, 3, 2):
            value = value + decode(r1.at[k, j])
        if k:
            encode(s2.at[k], value)
            sent[k] = net.copy(s2.at[k], r2.at[k], second[k])
        else:
            here[...] = value
        yield 1
    value = here[...]
    for k in (2, 1, 3):
        sent[k].wait_recv()
        value = value + decode(r2.at[k])
    total(value)


def sum_four(ref):
    return (ref[0] + ref[1]) + (ref[2] + ref[3])


def gram_rows(net, at, whole, four, two, full):
    block = (at.y * 4 + at.core * 2 + at.t) * 16
    four[at.z] = whole[pl.ds(pl.multiple_of(block, 16), 16), :]
    yield from spread(net, lambda p: four.at[p], at.z, at.dz[1:])
    two[0] = sum_four(four)
    yield from swap(net, at_step(two, 0), at_step(two, 1), at.dx[2])
    full[at.y, at.core, at.t] = two[0] + two[1]
    yield from swap(net, lambda: full.at[at.y, at.core, at.t], lambda: full.at[at.y, at.core, at.t], at.pair)
    yield from spread(net, lambda p: full.at[p, at.core], at.y, at.dy[1:])
    yield from swap(net, lambda: full.at[:, at.core], lambda: full.at[:, at.core], at.other)


def gram_cols(net, at, whole, four, two, full):
    block = (at.z * 4 + at.x) * 16
    four[at.y] = whole[pl.ds(pl.multiple_of(block, 16), 16), :]
    yield from spread(net, lambda p: four.at[p], at.y, at.dy[1:])
    two[0] = sum_four(four)
    yield from swap(net, at_step(two, 0), at_step(two, 1), at.other)
    full[at.z, at.x] = two[0] + two[1]
    yield from spread(net, lambda p: full.at[p, at.x], at.z, at.dz[1:])
    yield from spread(net, lambda p: full.at[:, p], at.x, at.dx[1:])


def reduce_time(net, at, part, four_y, two_y, four_z, two_z, total):
    four_y[at.y] = part[...]
    yield from spread(net, lambda p: four_y.at[p], at.y, at.dy[1:])
    two_y[0] = sum_four(four_y)
    yield from swap(net, at_step(two_y, 0), at_step(two_y, 1), at.other)
    four_z[at.z] = two_y[0] + two_y[1]
    yield from spread(net, lambda p: four_z.at[p], at.z, at.dz[1:])
    two_z[0] = sum_four(four_z)
    yield from swap(net, at_step(two_z, 0), at_step(two_z, 1), at.dx[2])
    total[...] = two_z[0] + two_z[1]


def exact_dot(left, right):
    high = right.astype(BF16)
    rest = right - high.astype(F32)
    mid = rest.astype(BF16)
    low = (rest - mid.astype(F32)).astype(BF16)
    return (
        jnp.dot(left, low, preferred_element_type=F32)
        + jnp.dot(left, mid, preferred_element_type=F32)
        + jnp.dot(left, high, preferred_element_type=F32)
    )


def gram(ref):
    block = ref[...]
    return lax.dot_general(block, block, (((0,), (0,)), ((), ())), preferred_element_type=F32)


def gradient_kernel(
    coords, count, values, rows, cols, times, grad_a, grad_b, grad_c, s, plan, send, recv, local
):
    at = Place()
    net = Net(send, recv)
    a_full, b_full, c_full = s["a"], s["b"], s["c"]
    a_flat = a_full.reshape(16, EDGE, RANK)
    b_flat = b_full.reshape(16, EDGE, RANK)
    held, prefix = s["held"], s["prefix"]
    own = [
        pltpu.make_async_copy(cols.at[0], b_full.at[at.z, at.x], local.at[0]),
        pltpu.make_async_copy(rows.at[0], a_full.at[at.y, at.core, at.t], local.at[1]),
        pltpu.make_async_copy(times, c_full.at[at.t], local.at[2]),
        pltpu.make_async_copy(coords, s["coords"], local.at[3]),
    ]
    for copy in own:
        copy.start()
    part = SLOTS // LOADS
    loads = [
        pltpu.make_async_copy(
            values.at[part * i : part * i + part], held.at[part * i : part * i + part], local.at[4 + i]
        )
        for i in range(LOADS)
    ]
    at.greet()
    bring_b = gather_cols(net, at, b_full, cols.at[0])
    bring_a = gather_rows(net, at, a_full, rows.at[0])
    bring_c = swap(net, times, c_full.at[at.t], at.pair)
    step(bring_a, bring_b, bring_c)
    for copy in loads:
        copy.start()
    for copy in own:
        copy.wait()

    s["times"][0:32] = jnp.zeros((32, RANK), F32)
    s["times"][32:64] = c_full[at.t].astype(F32)
    prefix[0] = jnp.zeros((EDGE, RANK), F32)
    s["dots"][PADDED:LANES] = jnp.zeros((LANES - PADDED, RANK), F32)
    for line in (1, 4, 6):
        s["plan"][line : line + 2] = jnp.zeros((2, LANES), jnp.int32)
    make_plan(s["plan"], s["coords"], count[0])
    tell = pltpu.make_async_copy(s["plan"], plan, local.at[4 + LOADS])
    tell.start()
    step(bring_a, bring_b)
    tell.wait()
    for copy in loads:
        copy.wait()
    step(bring_a)
    drive(bring_b, bring_a, bring_c)

    s["gram"][...] = gram(b_full.reshape(16 * EDGE, RANK))
    share_b = gram_cols(net, at, s["gram"], s["gb4"], s["gb2"], s["gb"])
    step(share_b)
    s["gram_a"][...] = gram(a_full.reshape(16 * EDGE, RANK))
    share_a = gram_rows(net, at, s["gram_a"], s["ga4"], s["ga2"], s["ga"])
    step(share_a)
    hooks = {5: lambda: step(share_b, share_a), 7: lambda: step(share_b)}
    tile_pass(
        plan, 0, held, s["times"], b_flat, False, prefix, hooks, a_flat, s["dots"]
    )

    def row_block(y, core, t):
        i = y * 4 + core * 2 + t
        return prefix[plan[2, i]] - prefix[plan[1, i]]

    part_a = reduce_rows(net, at, row_block, s["chip"], s["total_a"], s)
    step(part_a)
    snaps = s["plan"][0:1] >> 17
    pick = (snaps == iota((32, LANES), 0) + 32).astype(F32).astype(BF16)
    s["part_c"][...] = exact_dot(pick, s["dots"][...])
    part_c = reduce_time(
        net, at, s["part_c"], s["cy4"], s["cy2"], s["cz4"], s["cz2"], s["total_c"]
    )
    step(part_c)
    hooks = {
        1: lambda: step(share_a),
        2: lambda: step(share_b),
        4: lambda: step(part_a, share_a),
        5: lambda: step(part_c),
        7: lambda: step(part_c),
        9: lambda: step(share_b, share_a),
    }
    tile_pass(plan, 3, held, s["times"], a_flat, True, prefix, hooks)

    def col_block(z, x, h):
        i = z * 4 + x
        lanes = slice(128 * h, 128 * h + 128)
        return prefix[plan[5, i], :, lanes] - prefix[plan[4, i], :, lanes]

    def put(h):
        def total(value):
            s["total_b"][:, 128 * h : 128 * h + 128] = value

        return total

    part_b = [
        reduce_cols(
            net, lambda k, j: col_block(at.zs[k], at.xs[j], 0),
            at.dx, at.dz, s["here0"], put(0), s["s10"], s["r10"], s["s20"], s["r20"],
        ),
        reduce_cols(
            net, lambda k, j: col_block(at.zs[j], at.xs[k], 1),
            at.dz, at.dx, s["here1"], put(1), s["s11"], s["r11"], s["s21"], s["r21"],
        ),
    ]
    for _ in range(4):
        step(*part_b)
    step(share_a, part_c)
    whole_a = s["ga"][...].reshape(RANK, RANK)
    whole_b = s["gb"][...].reshape(RANK, RANK)
    whole_c = gram(c_full.reshape(64, RANK))
    s["near_a"][...] = exact_dot(a_full[at.y, at.core, at.t], whole_b * whole_c)
    s["near_b"][...] = exact_dot(b_full[at.z, at.x], whole_a * whole_c)
    step(*part_b)
    step(part_a)
    step(*part_b)
    step(*part_b)
    step(part_c)
    grad_c[...] = exact_dot(c_full[at.t], whole_a * whole_b) - s["total_c"][...]
    step(*part_b)
    step(part_a)
    grad_a[0] = s["near_a"][...] - s["total_a"][...]
    drive(*part_b)
    grad_b[0] = s["near_b"][...] - s["total_b"][...]
    net.close()


def hand_over(in_a, in_b, in_c, out_a, out_b, out_c, held_a, held_b, held_c, sems):
    path = ((in_a, held_a, out_a), (in_b, held_b, out_b), (in_c, held_c, out_c))
    bring = [pltpu.make_async_copy(p[0], p[1], sems.at[i]) for i, p in enumerate(path)]
    leave = [pltpu.make_async_copy(p[1], p[2], sems.at[3 + i]) for i, p in enumerate(path)]
    for copy in bring:
        copy.start()
    for came, gone in zip(bring, leave):
        came.wait()
        gone.start()
    for copy in leave:
        copy.wait()


def on_device(tile_values, tile_coords, tile_counts, factor_rows, factor_cols, factor_time):
    values = tile_values.reshape(SLOTS, EDGE, EDGE)
    coords = tile_coords.reshape(3, 1, SLOTS)
    count = tile_counts.reshape(1)
    wire = lambda *lead: pltpu.VMEM(lead + (RANK,), I16)
    half = lambda *lead: pltpu.VMEM(lead + (EDGE,), I16)
    real = lambda *lead: pltpu.VMEM(lead + (RANK,), F32)
    big = EDGE + PAD
    scratch = dict(
        a=pltpu.VMEM((4, 2, 2, EDGE, RANK), BF16),
        b=pltpu.VMEM((4, 4, EDGE, RANK), BF16),
        c=pltpu.VMEM((2, 32, RANK), BF16),
        held=pltpu.VMEM((SLOTS, EDGE, EDGE), BF16),
        prefix=real(ROUNDS + 1, EDGE),
        dots=real(LANES), times=real(64), part_c=real(32),
        plan=pltpu.VMEM((8, LANES), jnp.int32), coords=pltpu.VMEM((3, 1, SLOTS), jnp.int32),
        chip=real(4, 2, EDGE), total_a=real(EDGE), total_b=real(EDGE), total_c=real(32),
        core_s=wire(4, 2, big), core_r=wire(4, 2, big),
        y_s=wire(4, 2, big), y_r=wire(4, 2, big), x_s=wire(big), x_r=wire(big),
        s10=half(4, 4, big), r10=half(4, 4, big), s20=half(4, big), r20=half(4, big),
        s11=half(4, 4, big), r11=half(4, 4, big), s21=half(4, big), r21=half(4, big),
        here0=pltpu.VMEM((EDGE, EDGE), F32), here1=pltpu.VMEM((EDGE, EDGE), F32),
        gram=real(RANK), gram_a=real(RANK), near_a=real(EDGE), near_b=real(EDGE),
        ga4=real(4, 16), ga2=real(2, 16), ga=real(4, 2, 2, 16),
        gb4=real(4, 16), gb2=real(2, 16), gb=real(4, 4, 16),
        cy4=real(4, 32), cy2=real(2, 32), cz4=real(4, 32), cz2=real(2, 32),
    )
    smem = pl.BlockSpec(memory_space=pltpu.SMEM)
    anywhere = pl.BlockSpec(memory_space=pl.ANY)
    whole = pl.BlockSpec(memory_space=pltpu.VMEM)
    shapes = (
        jax.ShapeDtypeStruct((1, EDGE, RANK), F32),
        jax.ShapeDtypeStruct((1, EDGE, RANK), F32),
        jax.ShapeDtypeStruct((32, RANK), F32),
    )
    copies = 128
    grads = pl.pallas_call(
        gradient_kernel,
        out_shape=shapes,
        in_specs=[anywhere, smem] + [anywhere] * 4,
        out_specs=(whole,) * 3,
        scratch_shapes=[
            scratch,
            pltpu.SMEM((8, LANES), jnp.int32),
            pltpu.SemaphoreType.DMA((copies,)),
            pltpu.SemaphoreType.DMA((copies,)),
            pltpu.SemaphoreType.DMA((5 + LOADS,)),
        ],
        compiler_params=pltpu.CompilerParams(
            collective_id=0, has_side_effects=True, vmem_limit_bytes=60 << 20
        ),
        name="gradient",
    )(coords, count, values, factor_rows, factor_cols, factor_time)
    return pl.pallas_call(
        hand_over,
        out_shape=shapes,
        in_specs=[anywhere] * 3,
        out_specs=(anywhere,) * 3,
        scratch_shapes=[pltpu.VMEM(kind.shape, F32) for kind in shapes]
        + [pltpu.SemaphoreType.DMA((6,))],
        compiler_params=pltpu.CompilerParams(vmem_limit_bytes=60 << 20),
        name="hand_over",
    )(*grads)


def solution(mesh):
    return jax.shard_map(
        on_device,
        mesh=mesh,
        in_specs=(
            P("row", "col", "tm", None, None, None),
            P("row", "col", "tm", None, None),
            P("row", "col", "tm"),
            P("row", ("col", "tm"), None),
            P("col", ("row", "tm"), None),
            P("tm", None),
        ),
        out_specs=(P("row", ("col", "tm"), None), P("col", ("row", "tm"), None), P("tm", None)),
        check_vma=False,
    )
```

```python
from types import FunctionType

import jax
import jax.numpy as jnp
from jax import lax
from jax.experimental import pallas as pl
from jax.experimental.pallas import tpu as pltpu
from jax.sharding import PartitionSpec as P

F32 = jnp.float32
BF16 = jnp.bfloat16
I16 = jnp.int16
MESH = pl.DeviceIdType.MESH
EDGE = 128
RANK = 256
PAD = 16


class Copy:
    def __init__(self, src, dst, send, recv, device):
        self.src, self.dst, self.send, self.recv, self.device = src, dst, send, recv, device

    def made(self):
        return pltpu.make_async_remote_copy(
            src_ref=self.src() if isinstance(self.src, FunctionType) else self.src,
            dst_ref=self.dst() if isinstance(self.dst, FunctionType) else self.dst,
            send_sem=self.send(),
            recv_sem=self.recv(),
            device_id=self.device,
            device_id_type=MESH,
        )

    def wait_recv(self):
        self.made().wait_recv()

    def wait_send(self):
        self.made().wait_send()


class Net:
    def __init__(self, send, recv):
        self.send, self.recv, self.used, self.open = send, recv, 0, []

    def copy(self, src, dst, device):
        n = self.used
        copy = Copy(src, dst, lambda: self.send.at[n], lambda: self.recv.at[n], device)
        self.used += 1
        copy.made().start()
        self.open.append(copy)
        return copy

    def close(self):
        for copy in self.open:
            copy.wait_send()


class Place:
    def __init__(self):
        row, col, self.t = lax.axis_index("row"), lax.axis_index("col"), lax.axis_index("tm")
        self.z, self.y, self.core = row // 2, col // 2, col % 2
        self.x = (row % 2) * 2 + self.t
        self.far_t, self.far_core = 1 - self.t, 1 - self.core
        self.zs = [self.z] + [(self.z + k) % 4 for k in (1, 2, 3)]
        self.ys = [self.y] + [(self.y + k) % 4 for k in (1, 2, 3)]
        self.xs = [self.x] + [(self.x + k) % 4 for k in (1, 2, 3)]
        mine = (row, col, self.t)
        self.dz = [mine] + [(z * 2 + self.x // 2, col, self.t) for z in self.zs[1:]]
        self.dy = [mine] + [(row, y * 2 + self.core, self.t) for y in self.ys[1:]]
        self.dx = [mine] + [(self.z * 2 + x // 2, col, x % 2) for x in self.xs[1:]]
        self.other = (row, self.y * 2 + self.far_core, self.t)
        self.pair = (row, col, self.far_t)

    def greet(self):
        barrier = pltpu.get_barrier_semaphore()
        others = [self.other] + self.dz[1:] + self.dy[1:] + self.dx[1:]
        for device in others:
            pl.semaphore_signal(barrier, inc=1, device_id=device, device_id_type=MESH)
        pl.semaphore_wait(barrier, len(others))


def step(run, *more):
    for each in (run,) + more:
        next(each, None)


def drive(*runs):
    runs = list(runs)
    while runs:
        for run in list(runs):
            if next(run, None) is None:
                runs.remove(run)


def spread(net, view, me, devices):
    made = [net.copy(lambda: view(me), lambda: view(me), device) for device in devices]
    yield 1
    for copy in made:
        copy.wait_recv()


def swap(net, src, dst, device):
    made = net.copy(src, dst, device)
    yield 1
    made.wait_recv()


def encode(wire, value):
    rows = value.shape[0]
    top = jnp.max(jnp.abs(value), axis=0, keepdims=True)
    power = jnp.ceil(jnp.log2(jnp.maximum(top, 1e-30)))
    coded = jnp.clip(value * jnp.exp2(15.0 - power), -32767.0, 32767.0)
    wire[0:rows] = jnp.round(coded).astype(jnp.int32).astype(I16)
    power = jnp.broadcast_to(power, (PAD, value.shape[1]))
    wire[rows : rows + PAD] = power.astype(jnp.int32).astype(I16)


def decode(wire):
    rows = wire.shape[0] - PAD
    power = wire[rows : rows + PAD].astype(jnp.int32).astype(F32)[0:1]
    return wire[0:rows].astype(jnp.int32).astype(F32) * jnp.exp2(power - 15.0)


SLOTS = 384
ROUND = 2
PADDED = SLOTS + 16 * (ROUND - 1)
ROUNDS = PADDED // ROUND
LANES = 512
UNROLL = 40
LOADS = 12


def iota(shape, dim):
    return lax.broadcasted_iota(jnp.int32, shape, dim)


def up_to_round(n):
    return (n + (ROUND - 1)) // ROUND * ROUND


def lane_sum(value):
    return jnp.sum(value.astype(F32), axis=1, keepdims=True).astype(jnp.int32)


def plan_groups(plan, line, key_row, key_col, entry):
    lane = iota((1, 128), 1)
    count = jnp.sum((key_col == lane).astype(jnp.int32), axis=0, keepdims=True)
    padded = up_to_round(count)
    group = iota((16, 128), 0)
    held = jnp.zeros((16, 128), jnp.int32)
    for m in range(SLOTS // 128):
        held += (key_row[:, 128 * m : 128 * m + 128] == group).astype(jnp.int32)
    tall = up_to_round(lane_sum(held))
    end = jnp.sum(jnp.where(group <= iota((16, 128), 1), tall, 0), axis=0, keepdims=True)
    plan[line + 1 : line + 2, 0:128] = jnp.clip((end - padded) // ROUND, 0, ROUNDS)
    plan[line + 2 : line + 3, 0:128] = jnp.clip(end // ROUND, 0, ROUNDS)
    found = [jnp.zeros((1, 128), jnp.int32) for _ in range(LANES // 128)]
    for c in range(SLOTS // 128):
        mine = key_col[128 * c : 128 * c + 128]
        before = jnp.where(iota((128, 128), 1) < mine, padded, 0)
        for m in range(SLOTS // 128):
            same = key_row[:, 128 * m : 128 * m + 128] == mine
            earlier = iota((128, 128), 1) + 128 * m < iota((128, 128), 0) + 128 * c
            before += (same & earlier).astype(jnp.int32)
        place = lane_sum(before)
        told = entry[128 * c : 128 * c + 128]
        for q in range(LANES // 128):
            hit = place == iota((128, 128), 1) + 128 * q
            found[q] += jnp.sum(jnp.where(hit, told, 0), axis=0, keepdims=True)
    for q in range(LANES // 128):
        plan[line : line + 1, 128 * q : 128 * q + 128] = found[q]


def make_plan(plan, coords, live):
    rows, cols, snaps = coords[0], coords[1], coords[2]
    slot = iota((1, SLOTS), 1)
    row = jnp.where(slot < live, snaps + 32, 0)
    entry = slot + rows * 512 + cols * 8192 + row * 131072
    tall = jnp.concatenate(
        [jnp.broadcast_to(entry[:, 128 * c : 128 * c + 128], (128, 128)).T for c in range(3)],
        axis=0,
    )
    plan_groups(plan, 0, rows, (tall >> 9) & 15, tall)
    plan_groups(plan, 3, cols, (tall >> 13) & 15, tall)


def gather_rows(net, at, full, source):
    own = full.at[at.y, at.core, at.t]
    pair = net.copy(source, own, at.pair)
    mine = {k: net.copy(source, own, at.dy[k]) for k in (2, 1, 3)}
    yield 1
    pair.wait_recv()
    other = full.at[at.y, at.core, at.far_t]
    far = {k: net.copy(other, other, at.dy[k]) for k in (2, 1, 3)}
    near = full.at[at.y, at.core]
    across = [net.copy(near, near, at.other)]
    yield 1
    for k in (1, 3, 2):
        mine[k].wait_recv()
        far[k].wait_recv()
        came = full.at[at.ys[4 - k], at.core]
        across.append(net.copy(came, came, at.other))
    yield 1
    for copy in across:
        copy.wait_recv()


def gather_cols(net, at, full, source):
    def low(z):
        return full.at[z, at.x, 0:64]

    def high(x):
        return full.at[at.z, x, 64:128]

    order = (2, 1, 3)
    own_low, own_high = source.at[0:64], source.at[64:128]
    low_in, high_in, rest = {}, {}, []
    for k in order:
        low_in[k] = net.copy(own_low, low(at.z), at.dz[k])
        high_in[k] = net.copy(own_high, high(at.x), at.dx[k])
    for k in order:
        rest.append(net.copy(own_low, low(at.z), at.dx[k]))
        rest.append(net.copy(own_high, high(at.x), at.dz[k]))
    yield 1
    for k in (1, 3, 2):
        low_in[k].wait_recv()
        came = low(at.zs[4 - k])
        rest += [net.copy(came, came, at.dx[j]) for j in order]
        high_in[k].wait_recv()
        came = high(at.xs[4 - k])
        rest += [net.copy(came, came, at.dz[j]) for j in order]
    yield 1
    for copy in rest:
        copy.wait_recv()


def tile_pass(plan, line, held, times, operand, turned, prefix, hooks, other=None, dots=None):
    key = 13 if line == 0 else 9
    back = 9 if line == 0 else 13

    @pl.loop(0, PADDED // UNROLL)
    def _(trip):
        for when, hook in hooks.items():
            pl.when(trip == when)(hook)
        total = prefix[trip * (UNROLL // ROUND)]
        for j in range(UNROLL // ROUND):
            for u in range(ROUND):
                place = trip * UNROLL + j * ROUND + u
                entry = plan[line, place]
                tile = held[jnp.minimum(entry & 511, SLOTS - 1)]
                dims = (((0,), (0,)), ((), ())) if turned else (((1,), (0,)), ((), ()))
                prod = lax.dot_general(
                    tile, operand[(entry >> key) & 15], dims, preferred_element_type=F32
                )
                total = total + prod * times[pl.ds((entry >> 17) & 63, 1), :]
                if dots is not None:
                    facing = other[(entry >> back) & 15].astype(F32)
                    dots[pl.ds(place, 1), :] = jnp.sum(facing * prod, axis=0, keepdims=True)
            prefix[trip * (UNROLL // ROUND) + j + 1] = total


def at_step(ref, k):
    return lambda: ref.at[k]


def reduce_rows(net, at, block, chip, total, s):
    order = (2, 1, 3, 0)
    made = {}
    for k in order:
        for h in range(2):
            encode(s["core_s"].at[k, h], block(at.ys[k], at.far_core, h))
        made[k] = net.copy(at_step(s["core_s"], k), at_step(s["core_r"], k), at.other)
    for k in order:
        for h in range(2):
            chip[k, h] = block(at.ys[k], at.core, h)
    yield 1
    paired = {}
    for k in order:
        made[k].wait_recv()
        for h in range(2):
            chip[k, h] += decode(s["core_r"].at[k, h])
        encode(s["x_s"].at[k], chip[k, at.far_t])
        paired[k] = net.copy(at_step(s["x_s"], k), at_step(s["x_r"], k), at.pair)
    yield 1
    sent = {}
    for k in order:
        paired[k].wait_recv()
        value = chip[k, at.t] + decode(s["x_r"].at[k])
        if k:
            encode(s["y_s"].at[k], value)
            sent[k] = net.copy(at_step(s["y_s"], k), at_step(s["y_r"], k), at.dy[k])
        else:
            total[...] = value
    yield 1
    for k in (1, 3, 2):
        sent[k].wait_recv()
        total[...] += decode(s["y_r"].at[k])


def reduce_cols(net, block, first, second, here, total, s1, r1, s2, r2):
    order = (2, 1, 3, 0)
    made = {}
    for k in order:
        for j in (2, 1, 3):
            encode(s1.at[k, j], block(k, j))
            made[k, j] = net.copy(s1.at[k, j], r1.at[k, j], first[j])
        yield 1
    sent = {}
    for k in order:
        for j in (1, 3, 2):
            made[k, j].wait_recv()
        value = block(k, 0)
        for j in (1, 3, 2):
            value = value + decode(r1.at[k, j])
        if k:
            encode(s2.at[k], value)
            sent[k] = net.copy(s2.at[k], r2.at[k], second[k])
        else:
            here[...] = value
        yield 1
    value = here[...]
    for k in (2, 1, 3):
        sent[k].wait_recv()
        value = value + decode(r2.at[k])
    total(value)


def sum_four(ref):
    return (ref[0] + ref[1]) + (ref[2] + ref[3])


def gram_rows(net, at, whole, four, two, full):
    block = (at.y * 4 + at.core * 2 + at.t) * 16
    four[at.z] = whole[pl.ds(pl.multiple_of(block, 16), 16), :]
    yield from spread(net, lambda p: four.at[p], at.z, at.dz[1:])
    two[0] = sum_four(four)
    yield from swap(net, at_step(two, 0), at_step(two, 1), at.dx[2])
    full[at.y, at.core, at.t] = two[0] + two[1]
    yield from swap(net, lambda: full.at[at.y, at.core, at.t], lambda: full.at[at.y, at.core, at.t], at.pair)
    yield from spread(net, lambda p: full.at[p, at.core], at.y, at.dy[1:])
    yield from swap(net, lambda: full.at[:, at.core], lambda: full.at[:, at.core], at.other)


def gram_cols(net, at, whole, four, two, full):
    block = (at.z * 4 + at.x) * 16
    four[at.y] = whole[pl.ds(pl.multiple_of(block, 16), 16), :]
    yield from spread(net, lambda p: four.at[p], at.y, at.dy[1:])
    two[0] = sum_four(four)
    yield from swap(net, at_step(two, 0), at_step(two, 1), at.other)
    full[at.z, at.x] = two[0] + two[1]
    yield from spread(net, lambda p: full.at[p, at.x], at.z, at.dz[1:])
    yield from spread(net, lambda p: full.at[:, p], at.x, at.dx[1:])


def reduce_time(net, at, part, two_x, four_z, two_c, four_y, total):
    two_x[0] = part[...]
    yield from swap(net, at_step(two_x, 0), at_step(two_x, 1), at.dx[2])
    four_z[at.z] = two_x[0] + two_x[1]
    yield from spread(net, lambda p: four_z.at[p], at.z, at.dz[1:])
    two_c[0] = sum_four(four_z)
    yield from swap(net, at_step(two_c, 0), at_step(two_c, 1), at.other)
    four_y[at.y] = two_c[0] + two_c[1]
    yield from spread(net, lambda p: four_y.at[p], at.y, at.dy[1:])
    total[...] = sum_four(four_y)


def exact_dot(left, right):
    high = right.astype(BF16)
    rest = right - high.astype(F32)
    mid = rest.astype(BF16)
    low = (rest - mid.astype(F32)).astype(BF16)
    return (
        jnp.dot(left, low, preferred_element_type=F32)
        + jnp.dot(left, mid, preferred_element_type=F32)
        + jnp.dot(left, high, preferred_element_type=F32)
    )


def gram(ref):
    block = ref[...]
    return lax.dot_general(block, block, (((0,), (0,)), ((), ())), preferred_element_type=F32)


def gradient_kernel(
    coords, count, values, rows, cols, times, grad_a, grad_b, grad_c, s, plan, send, recv, local
):
    at = Place()
    net = Net(send, recv)
    a_full, b_full, c_full = s["a"], s["b"], s["c"]
    a_flat = a_full.reshape(16, EDGE, RANK)
    b_flat = b_full.reshape(16, EDGE, RANK)
    held, prefix = s["held"], s["prefix"]
    own = [
        pltpu.make_async_copy(cols.at[0], b_full.at[at.z, at.x], local.at[0]),
        pltpu.make_async_copy(rows.at[0], a_full.at[at.y, at.core, at.t], local.at[1]),
        pltpu.make_async_copy(times, c_full.at[at.t], local.at[2]),
        pltpu.make_async_copy(coords, s["coords"], local.at[3]),
    ]
    for copy in own:
        copy.start()
    part = SLOTS // LOADS
    loads = [
        pltpu.make_async_copy(
            values.at[part * i : part * i + part], held.at[part * i : part * i + part], local.at[4 + i]
        )
        for i in range(LOADS)
    ]
    at.greet()
    bring_b = gather_cols(net, at, b_full, cols.at[0])
    bring_a = gather_rows(net, at, a_full, rows.at[0])
    bring_c = swap(net, times, c_full.at[at.t], at.pair)
    step(bring_a, bring_b, bring_c)
    for copy in loads:
        copy.start()
    for copy in own:
        copy.wait()

    step(bring_a, bring_b)
    s["times"][0:32] = jnp.zeros((32, RANK), F32)
    s["times"][32:64] = c_full[at.t].astype(F32)
    prefix[0] = jnp.zeros((EDGE, RANK), F32)
    s["dots"][PADDED:LANES] = jnp.zeros((LANES - PADDED, RANK), F32)
    for line in (1, 4, 6):
        s["plan"][line : line + 2] = jnp.zeros((2, LANES), jnp.int32)
    make_plan(s["plan"], s["coords"], count[0])
    tell = pltpu.make_async_copy(s["plan"], plan, local.at[4 + LOADS])
    tell.start()
    step(bring_a)
    tell.wait()
    for copy in loads:
        copy.wait()
    drive(bring_b, bring_a, bring_c)

    s["gram"][...] = gram(b_full.reshape(16 * EDGE, RANK))
    share_b = gram_cols(net, at, s["gram"], s["gb4"], s["gb2"], s["gb"])
    step(share_b)
    s["gram_a"][...] = gram(a_full.reshape(16 * EDGE, RANK))
    share_a = gram_rows(net, at, s["gram_a"], s["ga4"], s["ga2"], s["ga"])
    step(share_a)
    hooks = {5: lambda: step(share_b, share_a), 7: lambda: step(share_b)}
    tile_pass(
        plan, 0, held, s["times"], b_flat, False, prefix, hooks, a_flat, s["dots"]
    )

    def row_block(y, core, t):
        i = y * 4 + core * 2 + t
        return prefix[plan[2, i]] - prefix[plan[1, i]]

    part_a = reduce_rows(net, at, row_block, s["chip"], s["total_a"], s)
    step(part_a)
    snaps = s["plan"][0:1] >> 17
    pick = (snaps == iota((32, LANES), 0) + 32).astype(F32).astype(BF16)
    s["part_c"][...] = exact_dot(pick, s["dots"][...])
    part_c = reduce_time(
        net, at, s["part_c"], s["cx2"], s["cz4"], s["cc2"], s["cy4"], s["total_c"]
    )
    step(part_c)
    hooks = {
        1: lambda: step(share_a),
        2: lambda: step(share_b),
        3: lambda: step(part_a),
        4: lambda: step(share_a),
        5: lambda: step(part_c),
        9: lambda: step(share_b, share_a, part_c),
    }
    tile_pass(plan, 3, held, s["times"], a_flat, True, prefix, hooks)

    def col_block(z, x, h):
        i = z * 4 + x
        lanes = slice(128 * h, 128 * h + 128)
        return prefix[plan[5, i], :, lanes] - prefix[plan[4, i], :, lanes]

    def put(h):
        def total(value):
            s["total_b"][:, 128 * h : 128 * h + 128] = value

        return total

    part_b = [
        reduce_cols(
            net, lambda k, j: col_block(at.zs[k], at.xs[j], 0),
            at.dx, at.dz, s["here0"], put(0), s["s10"], s["r10"], s["s20"], s["r20"],
        ),
        reduce_cols(
            net, lambda k, j: col_block(at.zs[j], at.xs[k], 1),
            at.dz, at.dx, s["here1"], put(1), s["s11"], s["r11"], s["s21"], s["r21"],
        ),
    ]
    for _ in range(4):
        step(*part_b)
    step(share_a, part_c, part_a)
    whole_a = s["ga"][...].reshape(RANK, RANK)
    whole_b = s["gb"][...].reshape(RANK, RANK)
    whole_c = gram(c_full.reshape(64, RANK))
    s["near_a"][...] = exact_dot(a_full[at.y, at.core, at.t], whole_b * whole_c)
    s["near_b"][...] = exact_dot(b_full[at.z, at.x], whole_a * whole_c)
    for _ in range(3):
        step(*part_b)
    step(part_c)
    grad_c[...] = exact_dot(c_full[at.t], whole_a * whole_b) - s["total_c"][...]
    step(*part_b)
    step(part_a)
    grad_a[0] = s["near_a"][...] - s["total_a"][...]
    drive(*part_b)
    grad_b[0] = s["near_b"][...] - s["total_b"][...]
    net.close()


def hand_over(in_a, in_b, in_c, out_a, out_b, out_c, held_a, held_b, held_c, sems):
    path = ((in_a, held_a, out_a), (in_b, held_b, out_b), (in_c, held_c, out_c))
    bring = [pltpu.make_async_copy(p[0], p[1], sems.at[i]) for i, p in enumerate(path)]
    leave = [pltpu.make_async_copy(p[1], p[2], sems.at[3 + i]) for i, p in enumerate(path)]
    for copy in bring:
        copy.start()
    for came, gone in zip(bring, leave):
        came.wait()
        gone.start()
    for copy in leave:
        copy.wait()


def on_device(tile_values, tile_coords, tile_counts, factor_rows, factor_cols, factor_time):
    values = tile_values.reshape(SLOTS, EDGE, EDGE)
    coords = tile_coords.reshape(3, 1, SLOTS)
    count = tile_counts.reshape(1)
    wire = lambda *lead: pltpu.VMEM(lead + (RANK,), I16)
    half = lambda *lead: pltpu.VMEM(lead + (EDGE,), I16)
    real = lambda *lead: pltpu.VMEM(lead + (RANK,), F32)
    big = EDGE + PAD
    scratch = dict(
        a=pltpu.VMEM((4, 2, 2, EDGE, RANK), BF16),
        b=pltpu.VMEM((4, 4, EDGE, RANK), BF16),
        c=pltpu.VMEM((2, 32, RANK), BF16),
        held=pltpu.VMEM((SLOTS, EDGE, EDGE), BF16),
        prefix=real(ROUNDS + 1, EDGE),
        dots=real(LANES), times=real(64), part_c=real(32),
        plan=pltpu.VMEM((8, LANES), jnp.int32), coords=pltpu.VMEM((3, 1, SLOTS), jnp.int32),
        chip=real(4, 2, EDGE), total_a=real(EDGE), total_b=real(EDGE), total_c=real(32),
        core_s=wire(4, 2, big), core_r=wire(4, 2, big),
        x_s=wire(4, big), x_r=wire(4, big), y_s=wire(4, big), y_r=wire(4, big),
        s10=half(4, 4, big), r10=half(4, 4, big), s20=half(4, big), r20=half(4, big),
        s11=half(4, 4, big), r11=half(4, 4, big), s21=half(4, big), r21=half(4, big),
        here0=pltpu.VMEM((EDGE, EDGE), F32), here1=pltpu.VMEM((EDGE, EDGE), F32),
        gram=real(RANK), gram_a=real(RANK), near_a=real(EDGE), near_b=real(EDGE),
        ga4=real(4, 16), ga2=real(2, 16), ga=real(4, 2, 2, 16),
        gb4=real(4, 16), gb2=real(2, 16), gb=real(4, 4, 16),
        cx2=real(2, 32), cz4=real(4, 32), cc2=real(2, 32), cy4=real(4, 32),
    )
    smem = pl.BlockSpec(memory_space=pltpu.SMEM)
    anywhere = pl.BlockSpec(memory_space=pl.ANY)
    whole = pl.BlockSpec(memory_space=pltpu.VMEM)
    shapes = (
        jax.ShapeDtypeStruct((1, EDGE, RANK), F32),
        jax.ShapeDtypeStruct((1, EDGE, RANK), F32),
        jax.ShapeDtypeStruct((32, RANK), F32),
    )
    copies = 128
    grads = pl.pallas_call(
        gradient_kernel,
        out_shape=shapes,
        in_specs=[anywhere, smem] + [anywhere] * 4,
        out_specs=(whole,) * 3,
        scratch_shapes=[
            scratch,
            pltpu.SMEM((8, LANES), jnp.int32),
            pltpu.SemaphoreType.DMA((copies,)),
            pltpu.SemaphoreType.DMA((copies,)),
            pltpu.SemaphoreType.DMA((5 + LOADS,)),
        ],
        compiler_params=pltpu.CompilerParams(
            collective_id=0, has_side_effects=True, vmem_limit_bytes=60 << 20
        ),
        name="gradient",
    )(coords, count, values, factor_rows, factor_cols, factor_time)
    return pl.pallas_call(
        hand_over,
        out_shape=shapes,
        in_specs=[anywhere] * 3,
        out_specs=(anywhere,) * 3,
        scratch_shapes=[pltpu.VMEM(kind.shape, F32) for kind in shapes]
        + [pltpu.SemaphoreType.DMA((6,))],
        compiler_params=pltpu.CompilerParams(vmem_limit_bytes=60 << 20),
        name="hand_over",
    )(*grads)


def solution(mesh):
    return jax.shard_map(
        on_device,
        mesh=mesh,
        in_specs=(
            P("row", "col", "tm", None, None, None),
            P("row", "col", "tm", None, None),
            P("row", "col", "tm"),
            P("row", ("col", "tm"), None),
            P("col", ("row", "tm"), None),
            P("tm", None),
        ),
        out_specs=(P("row", ("col", "tm"), None), P("col", ("row", "tm"), None), P("tm", None)),
        check_vma=False,
    )
```

```python
from types import FunctionType

import jax
import jax.numpy as jnp
from jax import lax
from jax.experimental import pallas as pl
from jax.experimental.pallas import tpu as pltpu
from jax.sharding import PartitionSpec as P

F32 = jnp.float32
BF16 = jnp.bfloat16
I16 = jnp.int16
MESH = pl.DeviceIdType.MESH
EDGE = 128
RANK = 256
PAD = 16


class Copy:
    def __init__(self, src, dst, send, recv, device):
        self.src, self.dst, self.send, self.recv, self.device = src, dst, send, recv, device

    def made(self):
        return pltpu.make_async_remote_copy(
            src_ref=self.src() if isinstance(self.src, FunctionType) else self.src,
            dst_ref=self.dst() if isinstance(self.dst, FunctionType) else self.dst,
            send_sem=self.send(),
            recv_sem=self.recv(),
            device_id=self.device,
            device_id_type=MESH,
        )

    def wait_recv(self):
        self.made().wait_recv()

    def wait_send(self):
        self.made().wait_send()


class Net:
    def __init__(self, send, recv):
        self.send, self.recv, self.used, self.open = send, recv, 0, []

    def copy(self, src, dst, device):
        n = self.used
        copy = Copy(src, dst, lambda: self.send.at[n], lambda: self.recv.at[n], device)
        self.used += 1
        copy.made().start()
        self.open.append(copy)
        return copy

    def close(self):
        for copy in self.open:
            copy.wait_send()


class Place:
    def __init__(self):
        row, col, self.t = lax.axis_index("row"), lax.axis_index("col"), lax.axis_index("tm")
        self.z, self.y, self.core = row // 2, col // 2, col % 2
        self.x = (row % 2) * 2 + self.t
        self.far_t, self.far_core = 1 - self.t, 1 - self.core
        self.zs = [self.z] + [(self.z + k) % 4 for k in (1, 2, 3)]
        self.ys = [self.y] + [(self.y + k) % 4 for k in (1, 2, 3)]
        self.xs = [self.x] + [(self.x + k) % 4 for k in (1, 2, 3)]
        mine = (row, col, self.t)
        self.dz = [mine] + [(z * 2 + self.x // 2, col, self.t) for z in self.zs[1:]]
        self.dy = [mine] + [(row, y * 2 + self.core, self.t) for y in self.ys[1:]]
        self.dx = [mine] + [(self.z * 2 + x // 2, col, x % 2) for x in self.xs[1:]]
        self.other = (row, self.y * 2 + self.far_core, self.t)
        self.pair = (row, col, self.far_t)

        self.others = [self.other] + self.dz[1:] + self.dy[1:] + self.dx[1:]

    def greet(self):
        barrier = pltpu.get_barrier_semaphore()
        for device in self.others:
            pl.semaphore_signal(barrier, inc=1, device_id=device, device_id_type=MESH)

    def await_all(self):
        pl.semaphore_wait(pltpu.get_barrier_semaphore(), len(self.others))


def step(run, *more):
    for each in (run,) + more:
        next(each, None)


def drive(*runs):
    runs = list(runs)
    while runs:
        for run in list(runs):
            if next(run, None) is None:
                runs.remove(run)


def spread(net, view, me, devices):
    made = [net.copy(lambda: view(me), lambda: view(me), device) for device in devices]
    yield 1
    for copy in made:
        copy.wait_recv()


def swap(net, src, dst, device):
    made = net.copy(src, dst, device)
    yield 1
    made.wait_recv()


SPAN = 14.9999
NEAREST = 12582912.0


def encode(wire, value):
    rows = value.shape[0]
    top = jnp.max(jnp.abs(value), axis=0, keepdims=True)
    power = jnp.ceil(jnp.log2(jnp.maximum(top, 1e-30)))
    coded = value * jnp.exp2(SPAN - power)
    wire[0:rows] = ((coded + NEAREST) - NEAREST).astype(jnp.int32).astype(I16)
    power = jnp.broadcast_to(power, (PAD, value.shape[1]))
    wire[rows : rows + PAD] = power.astype(jnp.int32).astype(I16)


def decode(wire):
    rows = wire.shape[0] - PAD
    power = wire[rows : rows + PAD].astype(jnp.int32).astype(F32)[0:1]
    return wire[0:rows].astype(jnp.int32).astype(F32) * jnp.exp2(power - SPAN)


SLOTS = 384
ROUND = 2
PADDED = SLOTS + 16 * (ROUND - 1)
ROUNDS = PADDED // ROUND
LANES = 512
UNROLL = 40
LOADS = 12


def iota(shape, dim):
    return lax.broadcasted_iota(jnp.int32, shape, dim)


def up_to_round(n):
    return (n + (ROUND - 1)) // ROUND * ROUND


def lane_sum(value):
    return jnp.sum(value.astype(F32), axis=1, keepdims=True).astype(jnp.int32)


def plan_groups(plan, line, key_row, key_col, entry):
    lane = iota((1, 128), 1)
    count = jnp.sum((key_col == lane).astype(jnp.int32), axis=0, keepdims=True)
    padded = up_to_round(count)
    group = iota((16, 128), 0)
    held = jnp.zeros((16, 128), jnp.int32)
    for m in range(SLOTS // 128):
        held += (key_row[:, 128 * m : 128 * m + 128] == group).astype(jnp.int32)
    tall = up_to_round(lane_sum(held))
    end = jnp.sum(jnp.where(group <= iota((16, 128), 1), tall, 0), axis=0, keepdims=True)
    plan[line + 1 : line + 2, 0:128] = jnp.clip((end - padded) // ROUND, 0, ROUNDS)
    plan[line + 2 : line + 3, 0:128] = jnp.clip(end // ROUND, 0, ROUNDS)
    found = [jnp.zeros((1, 128), jnp.int32) for _ in range(LANES // 128)]
    for c in range(SLOTS // 128):
        mine = key_col[128 * c : 128 * c + 128]
        before = jnp.where(iota((128, 128), 1) < mine, padded, 0)
        for m in range(SLOTS // 128):
            same = key_row[:, 128 * m : 128 * m + 128] == mine
            earlier = iota((128, 128), 1) + 128 * m < iota((128, 128), 0) + 128 * c
            before += (same & earlier).astype(jnp.int32)
        place = lane_sum(before)
        told = entry[128 * c : 128 * c + 128]
        for q in range(LANES // 128):
            hit = place == iota((128, 128), 1) + 128 * q
            found[q] += jnp.sum(jnp.where(hit, told, 0), axis=0, keepdims=True)
    for q in range(LANES // 128):
        plan[line : line + 1, 128 * q : 128 * q + 128] = found[q]


def make_plan(plan, coords, live):
    rows, cols, snaps = coords[0], coords[1], coords[2]
    slot = iota((1, SLOTS), 1)
    row = jnp.where(slot < live, snaps + 32, 0)
    entry = slot + rows * 512 + cols * 8192 + row * 131072
    tall = jnp.concatenate(
        [jnp.broadcast_to(entry[:, 128 * c : 128 * c + 128], (128, 128)).T for c in range(3)],
        axis=0,
    )
    plan_groups(plan, 0, rows, (tall >> 9) & 15, tall)
    plan_groups(plan, 3, cols, (tall >> 13) & 15, tall)


def gather_rows(net, at, full, source):
    own = full.at[at.y, at.core, at.t]
    pair = net.copy(source, own, at.pair)
    mine = {k: net.copy(source, own, at.dy[k]) for k in (2, 1, 3)}
    yield 1
    pair.wait_recv()
    other = full.at[at.y, at.core, at.far_t]
    far = {k: net.copy(other, other, at.dy[k]) for k in (2, 1, 3)}
    near = full.at[at.y, at.core]
    across = [net.copy(near, near, at.other)]
    yield 1
    for k in (1, 3, 2):
        mine[k].wait_recv()
        far[k].wait_recv()
        came = full.at[at.ys[4 - k], at.core]
        across.append(net.copy(came, came, at.other))
    yield 1
    for copy in across:
        copy.wait_recv()


def gather_cols(net, at, full, source):
    def low(z):
        return full.at[z, at.x, 0:64]

    def high(x):
        return full.at[at.z, x, 64:128]

    order = (2, 1, 3)
    own_low, own_high = source.at[0:64], source.at[64:128]
    low_in, high_in, rest = {}, {}, []
    for k in order:
        low_in[k] = net.copy(own_low, low(at.z), at.dz[k])
        high_in[k] = net.copy(own_high, high(at.x), at.dx[k])
    for k in order:
        rest.append(net.copy(own_low, low(at.z), at.dx[k]))
        rest.append(net.copy(own_high, high(at.x), at.dz[k]))
    yield 1
    for k in (1, 3, 2):
        low_in[k].wait_recv()
        came = low(at.zs[4 - k])
        rest += [net.copy(came, came, at.dx[j]) for j in order]
        high_in[k].wait_recv()
        came = high(at.xs[4 - k])
        rest += [net.copy(came, came, at.dz[j]) for j in order]
    yield 1
    for copy in rest:
        copy.wait_recv()


def tile_pass(plan, line, held, times, operand, turned, prefix, hooks, other=None, dots=None):
    key = 13 if line == 0 else 9
    back = 9 if line == 0 else 13

    @pl.loop(0, PADDED // UNROLL)
    def _(trip):
        for when, hook in hooks.items():
            pl.when(trip == when)(hook)
        total = prefix[trip * (UNROLL // ROUND)]
        for j in range(UNROLL // ROUND):
            for u in range(ROUND):
                place = trip * UNROLL + j * ROUND + u
                entry = plan[line, place]
                tile = held[jnp.minimum(entry & 511, SLOTS - 1)]
                dims = (((0,), (0,)), ((), ())) if turned else (((1,), (0,)), ((), ()))
                prod = lax.dot_general(
                    tile, operand[(entry >> key) & 15], dims, preferred_element_type=F32
                )
                total = total + prod * times[pl.ds((entry >> 17) & 63, 1), :]
                if dots is not None:
                    facing = other[(entry >> back) & 15].astype(F32)
                    dots[pl.ds(place, 1), :] = jnp.sum(facing * prod, axis=0, keepdims=True)
            prefix[trip * (UNROLL // ROUND) + j + 1] = total


def at_step(ref, k):
    return lambda: ref.at[k]


def reduce_rows(net, at, block, chip, total, s):
    order = (2, 1, 3, 0)
    made = {}
    for k in order:
        for h in range(2):
            encode(s["core_s"].at[k, h], block(at.ys[k], at.far_core, h))
    for k in order:
        made[k] = net.copy(at_step(s["core_s"], k), at_step(s["core_r"], k), at.other)
    for k in order:
        for h in range(2):
            chip[k, h] = block(at.ys[k], at.core, h)
    yield 1
    sent = {}
    for k in order:
        made[k].wait_recv()
    for k in order:
        for h in range(2):
            value = chip[k, h] + decode(s["core_r"].at[k, h])
            if k:
                encode(s["y_s"].at[k, h], value)
            else:
                chip[0, h] = value
    for k in (2, 1, 3):
        sent[k] = net.copy(at_step(s["y_s"], k), at_step(s["y_r"], k), at.dy[k])
    yield 1
    for k in (1, 3, 2):
        sent[k].wait_recv()
    for h in range(2):
        value = chip[0, h]
        for k in (1, 3, 2):
            value = value + decode(s["y_r"].at[k, h])
        chip[0, h] = value
    encode(s["x_s"], chip[0, at.far_t])
    yield from swap(net, s["x_s"], s["x_r"], at.pair)
    total[...] = chip[0, at.t] + decode(s["x_r"])


def reduce_cols(net, at, block, here, total, s):
    order = (2, 1, 3, 0)
    ways = ((at.dx, at.dz), (at.dz, at.dx))
    part = (lambda k, j: block(k, j, 0), lambda k, j: block(j, k, 1))
    s1, r1 = (s["s10"], s["s11"]), (s["r10"], s["r11"])
    s2, r2 = (s["s20"], s["s21"]), (s["r20"], s["r21"])
    made, sent = {}, {}
    for k in order:
        for j in (2, 1, 3):
            for h in range(2):
                encode(s1[h].at[k, j], part[h](k, j))
        for j in (2, 1, 3):
            for h in range(2):
                made[h, k, j] = net.copy(s1[h].at[k, j], r1[h].at[k, j], ways[h][0][j])
        yield 1
    for k in order:
        for j in (1, 3, 2):
            for h in range(2):
                made[h, k, j].wait_recv()
        for h in range(2):
            value = part[h](k, 0)
            for j in (1, 3, 2):
                value = value + decode(r1[h].at[k, j])
            if k:
                encode(s2[h].at[k], value)
            else:
                here[h] = value
        for h in range(2):
            if k:
                sent[h, k] = net.copy(s2[h].at[k], r2[h].at[k], ways[h][1][k])
        yield 1
    for k in (2, 1, 3):
        for h in range(2):
            sent[h, k].wait_recv()
    for h in range(2):
        value = here[h]
        for k in (2, 1, 3):
            value = value + decode(r2[h].at[k])
        total[:, 128 * h : 128 * h + 128] = value


def sum_four(ref):
    return (ref[0] + ref[1]) + (ref[2] + ref[3])


def gram_rows(net, at, whole, four, two, full):
    block = (at.y * 4 + at.core * 2 + at.t) * 16
    four[at.z] = whole[pl.ds(pl.multiple_of(block, 16), 16), :]
    yield from spread(net, lambda p: four.at[p], at.z, at.dz[1:])
    two[0] = sum_four(four)
    yield from swap(net, at_step(two, 0), at_step(two, 1), at.dx[2])
    full[at.y, at.core, at.t] = two[0] + two[1]
    yield from spread(net, lambda p: full.at[p, at.core, at.t], at.y, at.dy[1:])
    column = lambda: full.at[:, at.core, at.t]
    yield from swap(net, column, column, at.pair)
    yield from swap(net, lambda: full.at[:, at.core], lambda: full.at[:, at.core], at.other)


def gram_cols(net, at, whole, four, two, full):
    block = (at.z * 4 + at.x) * 16
    four[at.y] = whole[pl.ds(pl.multiple_of(block, 16), 16), :]
    yield from spread(net, lambda p: four.at[p], at.y, at.dy[1:])
    two[0] = sum_four(four)
    yield from swap(net, at_step(two, 0), at_step(two, 1), at.other)
    full[at.z, at.x] = two[0] + two[1]
    yield from spread(net, lambda p: full.at[at.z, p], at.x, at.dx[1:])
    yield from spread(net, lambda p: full.at[p], at.z, at.dz[1:])


def reduce_time(net, at, part, two_x, four_z, two_c, four_y, total):
    two_x[0] = part[...]
    yield from swap(net, at_step(two_x, 0), at_step(two_x, 1), at.dx[2])
    four_z[at.z] = two_x[0] + two_x[1]
    yield from spread(net, lambda p: four_z.at[p], at.z, at.dz[1:])
    two_c[0] = sum_four(four_z)
    yield from swap(net, at_step(two_c, 0), at_step(two_c, 1), at.other)
    four_y[at.y] = two_c[0] + two_c[1]
    yield from spread(net, lambda p: four_y.at[p], at.y, at.dy[1:])
    total[...] = sum_four(four_y)


def exact_dot(left, right):
    high = right.astype(BF16)
    rest = right - high.astype(F32)
    mid = rest.astype(BF16)
    low = (rest - mid.astype(F32)).astype(BF16)
    return (
        jnp.dot(left, low, preferred_element_type=F32)
        + jnp.dot(left, mid, preferred_element_type=F32)
        + jnp.dot(left, high, preferred_element_type=F32)
    )


def gram(ref):
    block = ref[...]
    return lax.dot_general(block, block, (((0,), (0,)), ((), ())), preferred_element_type=F32)


def gradient_kernel(
    coords, count, values, rows, cols, times, grad_a, grad_b, grad_c, s, plan, send, recv, local
):
    at = Place()
    at.greet()
    net = Net(send, recv)
    a_full, b_full, c_full = s["a"], s["b"], s["c"]
    a_flat = a_full.reshape(16, EDGE, RANK)
    b_flat = b_full.reshape(16, EDGE, RANK)
    held, prefix = s["held"], s["prefix"]
    own = [
        pltpu.make_async_copy(cols.at[0], b_full.at[at.z, at.x], local.at[0]),
        pltpu.make_async_copy(rows.at[0], a_full.at[at.y, at.core, at.t], local.at[1]),
        pltpu.make_async_copy(times, c_full.at[at.t], local.at[2]),
        pltpu.make_async_copy(coords, s["coords"], local.at[3]),
    ]
    for copy in own:
        copy.start()
    part = SLOTS // LOADS
    loads = [
        pltpu.make_async_copy(
            values.at[part * i : part * i + part], held.at[part * i : part * i + part], local.at[4 + i]
        )
        for i in range(LOADS)
    ]
    at.await_all()
    bring_b = gather_cols(net, at, b_full, cols.at[0])
    bring_a = gather_rows(net, at, a_full, rows.at[0])
    bring_c = swap(net, times, c_full.at[at.t], at.pair)
    step(bring_a, bring_b, bring_c)
    for copy in loads:
        copy.start()
    for copy in own:
        copy.wait()

    step(bring_a, bring_b)
    s["times"][0:32] = jnp.zeros((32, RANK), F32)
    s["times"][32:64] = c_full[at.t].astype(F32)
    prefix[0] = jnp.zeros((EDGE, RANK), F32)
    s["dots"][PADDED:LANES] = jnp.zeros((LANES - PADDED, RANK), F32)
    for line in (1, 4, 6):
        s["plan"][line : line + 2] = jnp.zeros((2, LANES), jnp.int32)
    make_plan(s["plan"], s["coords"], count[0])
    tell = pltpu.make_async_copy(s["plan"], plan, local.at[4 + LOADS])
    tell.start()
    step(bring_a)
    tell.wait()
    for copy in loads:
        copy.wait()
    drive(bring_b, bring_c)
    s["gram"][...] = gram(b_full.reshape(16 * EDGE, RANK))
    share_b = gram_cols(net, at, s["gram"], s["gb4"], s["gb2"], s["gb"])
    step(share_b)
    drive(bring_a)
    s["gram_a"][...] = gram(a_full.reshape(16 * EDGE, RANK))
    share_a = gram_rows(net, at, s["gram_a"], s["ga4"], s["ga2"], s["ga"])
    step(share_a)
    hooks = {5: lambda: step(share_b, share_a), 7: lambda: step(share_b)}
    tile_pass(
        plan, 0, held, s["times"], b_flat, False, prefix, hooks, a_flat, s["dots"]
    )

    def row_block(y, core, t):
        i = y * 4 + core * 2 + t
        return prefix[plan[2, i]] - prefix[plan[1, i]]

    part_a = reduce_rows(net, at, row_block, s["chip"], s["total_a"], s)
    step(part_a)
    snaps = s["plan"][0:1] >> 17
    pick = (snaps == iota((32, LANES), 0) + 32).astype(F32).astype(BF16)
    s["part_c"][...] = exact_dot(pick, s["dots"][...])
    part_c = reduce_time(
        net, at, s["part_c"], s["cx2"], s["cz4"], s["cc2"], s["cy4"], s["total_c"]
    )
    step(part_c)
    hooks = {
        1: lambda: step(share_a),
        2: lambda: step(share_b),
        3: lambda: step(part_a),
        5: lambda: step(part_c),
        6: lambda: step(share_a),
        9: lambda: step(share_b, share_a, part_c),
    }
    tile_pass(plan, 3, held, s["times"], a_flat, True, prefix, hooks)

    def col_block(z, x, h):
        i = at.zs[z] * 4 + at.xs[x]
        lanes = slice(128 * h, 128 * h + 128)
        return prefix[plan[5, i], :, lanes] - prefix[plan[4, i], :, lanes]

    part_b = reduce_cols(net, at, col_block, s["here"], s["total_b"], s)
    for _ in range(4):
        step(part_b)
    step(share_a, part_c)
    whole_a = s["ga"][...].reshape(RANK, RANK)
    whole_b = s["gb"][...].reshape(RANK, RANK)
    whole_c = gram(c_full.reshape(64, RANK))
    s["near_a"][...] = exact_dot(a_full[at.y, at.core, at.t], whole_b * whole_c)
    s["near_b"][...] = exact_dot(b_full[at.z, at.x], whole_a * whole_c)
    step(part_b)
    step(part_a)
    for _ in range(2):
        step(part_b)
    step(part_c)
    s["out_c"][...] = exact_dot(c_full[at.t], whole_a * whole_b) - s["total_c"][...]
    gone_c = pltpu.make_async_copy(s["out_c"], grad_c, local.at[0])
    gone_c.start()
    step(part_b)
    step(part_a)
    s["near_a"][...] = s["near_a"][...] - s["total_a"][...]
    gone_a = pltpu.make_async_copy(s["near_a"], grad_a.at[0], local.at[1])
    gone_a.start()
    drive(part_b)
    s["near_b"][...] = s["near_b"][...] - s["total_b"][...]
    gone_b = pltpu.make_async_copy(s["near_b"], grad_b.at[0], local.at[2])
    gone_b.start()
    net.close()
    for copy in (gone_a, gone_b, gone_c):
        copy.wait()


def hand_over(in_a, in_b, in_c, out_a, out_b, out_c, held_a, held_b, held_c, sems):
    path = ((in_a, held_a, out_a), (in_b, held_b, out_b), (in_c, held_c, out_c))
    bring = [pltpu.make_async_copy(p[0], p[1], sems.at[i]) for i, p in enumerate(path)]
    leave = [pltpu.make_async_copy(p[1], p[2], sems.at[3 + i]) for i, p in enumerate(path)]
    for copy in bring:
        copy.start()
    for came, gone in zip(bring, leave):
        came.wait()
        gone.start()
    for copy in leave:
        copy.wait()


def on_device(tile_values, tile_coords, tile_counts, factor_rows, factor_cols, factor_time):
    values = tile_values.reshape(SLOTS, EDGE, EDGE)
    coords = tile_coords.reshape(3, 1, SLOTS)
    count = tile_counts.reshape(1)
    wire = lambda *lead: pltpu.VMEM(lead + (RANK,), I16)
    half = lambda *lead: pltpu.VMEM(lead + (EDGE,), I16)
    real = lambda *lead: pltpu.VMEM(lead + (RANK,), F32)
    big = EDGE + PAD
    scratch = dict(
        a=pltpu.VMEM((4, 2, 2, EDGE, RANK), BF16),
        b=pltpu.VMEM((4, 4, EDGE, RANK), BF16),
        c=pltpu.VMEM((2, 32, RANK), BF16),
        held=pltpu.VMEM((SLOTS, EDGE, EDGE), BF16),
        prefix=real(ROUNDS + 1, EDGE),
        dots=real(LANES), times=real(64), part_c=real(32),
        plan=pltpu.VMEM((8, LANES), jnp.int32), coords=pltpu.VMEM((3, 1, SLOTS), jnp.int32),
        chip=real(4, 2, EDGE), total_a=real(EDGE), total_b=real(EDGE), total_c=real(32),
        core_s=wire(4, 2, big), core_r=wire(4, 2, big),
        y_s=wire(4, 2, big), y_r=wire(4, 2, big), x_s=wire(big), x_r=wire(big),
        s10=half(4, 4, big), r10=half(4, 4, big), s20=half(4, big), r20=half(4, big),
        s11=half(4, 4, big), r11=half(4, 4, big), s21=half(4, big), r21=half(4, big),
        here=pltpu.VMEM((2, EDGE, EDGE), F32),
        gram=real(RANK), gram_a=real(RANK), near_a=real(EDGE), near_b=real(EDGE), out_c=real(32),
        ga4=real(4, 16), ga2=real(2, 16), ga=real(4, 2, 2, 16),
        gb4=real(4, 16), gb2=real(2, 16), gb=real(4, 4, 16),
        cx2=real(2, 32), cz4=real(4, 32), cc2=real(2, 32), cy4=real(4, 32),
    )
    smem = pl.BlockSpec(memory_space=pltpu.SMEM)
    anywhere = pl.BlockSpec(memory_space=pl.ANY)
    shapes = (
        jax.ShapeDtypeStruct((1, EDGE, RANK), F32),
        jax.ShapeDtypeStruct((1, EDGE, RANK), F32),
        jax.ShapeDtypeStruct((32, RANK), F32),
    )
    copies = 128
    grads = pl.pallas_call(
        gradient_kernel,
        out_shape=shapes,
        in_specs=[anywhere, smem] + [anywhere] * 4,
        out_specs=(anywhere,) * 3,
        scratch_shapes=[
            scratch,
            pltpu.SMEM((8, LANES), jnp.int32),
            pltpu.SemaphoreType.DMA((copies,)),
            pltpu.SemaphoreType.DMA((copies,)),
            pltpu.SemaphoreType.DMA((5 + LOADS,)),
        ],
        compiler_params=pltpu.CompilerParams(
            collective_id=0, has_side_effects=True, vmem_limit_bytes=60 << 20
        ),
        name="gradient",
    )(coords, count, values, factor_rows, factor_cols, factor_time)
    return pl.pallas_call(
        hand_over,
        out_shape=shapes,
        in_specs=[anywhere] * 3,
        out_specs=(anywhere,) * 3,
        scratch_shapes=[pltpu.VMEM(kind.shape, F32) for kind in shapes]
        + [pltpu.SemaphoreType.DMA((6,))],
        compiler_params=pltpu.CompilerParams(vmem_limit_bytes=60 << 20),
        name="hand_over",
    )(*grads)


def solution(mesh):
    return jax.shard_map(
        on_device,
        mesh=mesh,
        in_specs=(
            P("row", "col", "tm", None, None, None),
            P("row", "col", "tm", None, None),
            P("row", "col", "tm"),
            P("row", ("col", "tm"), None),
            P("col", ("row", "tm"), None),
            P("tm", None),
        ),
        out_specs=(P("row", ("col", "tm"), None), P("col", ("row", "tm"), None), P("tm", None)),
        check_vma=False,
    )
```

```python
from types import FunctionType

import jax
import jax.numpy as jnp
from jax import lax
from jax.experimental import pallas as pl
from jax.experimental.pallas import tpu as pltpu
from jax.sharding import PartitionSpec as P

F32 = jnp.float32
BF16 = jnp.bfloat16
I16 = jnp.int16
MESH = pl.DeviceIdType.MESH
EDGE = 128
RANK = 256
PAD = 16


class Copy:
    def __init__(self, src, dst, send, recv, device):
        self.src, self.dst, self.send, self.recv, self.device = src, dst, send, recv, device

    def made(self):
        return pltpu.make_async_remote_copy(
            src_ref=self.src() if isinstance(self.src, FunctionType) else self.src,
            dst_ref=self.dst() if isinstance(self.dst, FunctionType) else self.dst,
            send_sem=self.send(),
            recv_sem=self.recv(),
            device_id=self.device,
            device_id_type=MESH,
        )

    def wait_recv(self):
        self.made().wait_recv()

    def wait_send(self):
        self.made().wait_send()


class Net:
    def __init__(self, send, recv):
        self.send, self.recv, self.used, self.open = send, recv, 0, []

    def copy(self, src, dst, device):
        n = self.used
        copy = Copy(src, dst, lambda: self.send.at[n], lambda: self.recv.at[n], device)
        self.used += 1
        copy.made().start()
        self.open.append(copy)
        return copy

    def close(self):
        for copy in self.open:
            copy.wait_send()


class Place:
    def __init__(self):
        row, col, self.t = lax.axis_index("row"), lax.axis_index("col"), lax.axis_index("tm")
        self.z, self.y, self.core = row // 2, col // 2, col % 2
        self.x = (row % 2) * 2 + self.t
        self.far_t, self.far_core = 1 - self.t, 1 - self.core
        self.zs = [self.z] + [(self.z + k) % 4 for k in (1, 2, 3)]
        self.ys = [self.y] + [(self.y + k) % 4 for k in (1, 2, 3)]
        self.xs = [self.x] + [(self.x + k) % 4 for k in (1, 2, 3)]
        mine = (row, col, self.t)
        self.dz = [mine] + [(z * 2 + self.x // 2, col, self.t) for z in self.zs[1:]]
        self.dy = [mine] + [(row, y * 2 + self.core, self.t) for y in self.ys[1:]]
        self.dx = [mine] + [(self.z * 2 + x // 2, col, x % 2) for x in self.xs[1:]]
        self.other = (row, self.y * 2 + self.far_core, self.t)
        self.pair = (row, col, self.far_t)

        self.others = [self.other] + self.dz[1:] + self.dy[1:] + self.dx[1:]

    def greet(self):
        barrier = pltpu.get_barrier_semaphore()
        for device in self.others:
            pl.semaphore_signal(barrier, inc=1, device_id=device, device_id_type=MESH)

    def await_all(self):
        pl.semaphore_wait(pltpu.get_barrier_semaphore(), len(self.others))


def step(run, *more):
    for each in (run,) + more:
        next(each, None)


def drive(*runs):
    runs = list(runs)
    while runs:
        for run in list(runs):
            if next(run, None) is None:
                runs.remove(run)


def spread(net, view, me, devices):
    made = [net.copy(lambda: view(me), lambda: view(me), device) for device in devices]
    yield 1
    for copy in made:
        copy.wait_recv()


def swap(net, src, dst, device):
    made = net.copy(src, dst, device)
    yield 1
    made.wait_recv()


SPAN = 14.9999
NEAREST = 12582912.0


def encode(wire, value):
    rows = value.shape[0]
    top = jnp.max(jnp.abs(value), axis=0, keepdims=True)
    power = jnp.ceil(jnp.log2(jnp.maximum(top, 1e-30)))
    coded = value * jnp.exp2(SPAN - power)
    wire[0:rows] = ((coded + NEAREST) - NEAREST).astype(jnp.int32).astype(I16)
    power = jnp.broadcast_to(power, (PAD, value.shape[1]))
    wire[rows : rows + PAD] = power.astype(jnp.int32).astype(I16)


def decode(wire):
    rows = wire.shape[0] - PAD
    power = wire[rows : rows + PAD].astype(jnp.int32).astype(F32)[0:1]
    return wire[0:rows].astype(jnp.int32).astype(F32) * jnp.exp2(power - SPAN)


SLOTS = 384
ROUND = 2
PADDED = SLOTS + 16 * (ROUND - 1)
ROUNDS = PADDED // ROUND
LANES = 512
UNROLL = 80
LOADS = 12


def iota(shape, dim):
    return lax.broadcasted_iota(jnp.int32, shape, dim)


def up_to_round(n):
    return (n + (ROUND - 1)) // ROUND * ROUND


def lane_sum(value):
    return jnp.sum(value.astype(F32), axis=1, keepdims=True).astype(jnp.int32)


def plan_groups(plan, line, key_row, key_col, entry):
    lane = iota((1, 128), 1)
    count = jnp.sum((key_col == lane).astype(jnp.int32), axis=0, keepdims=True)
    padded = up_to_round(count)
    group = iota((16, 128), 0)
    held = jnp.zeros((16, 128), jnp.int32)
    for m in range(SLOTS // 128):
        held += (key_row[:, 128 * m : 128 * m + 128] == group).astype(jnp.int32)
    tall = up_to_round(lane_sum(held))
    end = jnp.sum(jnp.where(group <= iota((16, 128), 1), tall, 0), axis=0, keepdims=True)
    plan[line + 1 : line + 2, 0:128] = jnp.clip((end - padded) // ROUND, 0, ROUNDS)
    plan[line + 2 : line + 3, 0:128] = jnp.clip(end // ROUND, 0, ROUNDS)
    found = [jnp.zeros((1, 128), jnp.int32) for _ in range(LANES // 128)]
    for c in range(SLOTS // 128):
        mine = key_col[128 * c : 128 * c + 128]
        before = jnp.where(iota((128, 128), 1) < mine, padded, 0)
        for m in range(SLOTS // 128):
            same = key_row[:, 128 * m : 128 * m + 128] == mine
            earlier = iota((128, 128), 1) + 128 * m < iota((128, 128), 0) + 128 * c
            before += (same & earlier).astype(jnp.int32)
        place = lane_sum(before)
        told = entry[128 * c : 128 * c + 128]
        for q in range(LANES // 128):
            hit = place == iota((128, 128), 1) + 128 * q
            found[q] += jnp.sum(jnp.where(hit, told, 0), axis=0, keepdims=True)
    for q in range(LANES // 128):
        plan[line : line + 1, 128 * q : 128 * q + 128] = found[q]


def make_plan(plan, coords, live):
    rows, cols, snaps = coords[0], coords[1], coords[2]
    slot = iota((1, SLOTS), 1)
    row = jnp.where(slot < live, snaps + 32, 0)
    entry = slot + rows * 512 + cols * 8192 + row * 131072
    tall = jnp.concatenate(
        [jnp.broadcast_to(entry[:, 128 * c : 128 * c + 128], (128, 128)).T for c in range(3)],
        axis=0,
    )
    plan_groups(plan, 0, rows, (tall >> 9) & 15, tall)
    plan_groups(plan, 3, cols, (tall >> 13) & 15, tall)


def gather_rows(net, at, full, source):
    own = full.at[at.y, at.core, at.t]
    pair = net.copy(source, own, at.pair)
    mine = {k: net.copy(source, own, at.dy[k]) for k in (2, 1, 3)}
    yield 1
    pair.wait_recv()
    other = full.at[at.y, at.core, at.far_t]
    far = {k: net.copy(other, other, at.dy[k]) for k in (2, 1, 3)}
    near = full.at[at.y, at.core]
    across = [net.copy(near, near, at.other)]
    yield 1
    for k in (1, 3, 2):
        mine[k].wait_recv()
        far[k].wait_recv()
        came = full.at[at.ys[4 - k], at.core]
        across.append(net.copy(came, came, at.other))
    yield 1
    for copy in across:
        copy.wait_recv()


def gather_cols(net, at, full, source):
    def low(z):
        return full.at[z, at.x, 0:64]

    def high(x):
        return full.at[at.z, x, 64:128]

    order = (2, 1, 3)
    own_low, own_high = source.at[0:64], source.at[64:128]
    low_in, high_in, rest = {}, {}, []
    for k in order:
        low_in[k] = net.copy(own_low, low(at.z), at.dz[k])
        high_in[k] = net.copy(own_high, high(at.x), at.dx[k])
    for k in order:
        rest.append(net.copy(own_low, low(at.z), at.dx[k]))
        rest.append(net.copy(own_high, high(at.x), at.dz[k]))
    yield 1
    for k in (1, 3, 2):
        low_in[k].wait_recv()
        came = low(at.zs[4 - k])
        rest += [net.copy(came, came, at.dx[j]) for j in order]
        high_in[k].wait_recv()
        came = high(at.xs[4 - k])
        rest += [net.copy(came, came, at.dz[j]) for j in order]
    yield 1
    for copy in rest:
        copy.wait_recv()


def tile_pass(plan, line, held, times, operand, turned, prefix, hooks, other=None, dots=None):
    key = 13 if line == 0 else 9
    back = 9 if line == 0 else 13

    @pl.loop(0, PADDED // UNROLL)
    def _(trip):
        for when, hook in hooks.items():
            pl.when(trip == when)(hook)
        total = prefix[trip * (UNROLL // ROUND)]
        for j in range(UNROLL // ROUND):
            for u in range(ROUND):
                place = trip * UNROLL + j * ROUND + u
                entry = plan[line, place]
                tile = held[jnp.minimum(entry & 511, SLOTS - 1)]
                dims = (((0,), (0,)), ((), ())) if turned else (((1,), (0,)), ((), ()))
                prod = lax.dot_general(
                    tile, operand[(entry >> key) & 15], dims, preferred_element_type=F32
                )
                total = total + prod * times[pl.ds((entry >> 17) & 63, 1), :]
                if dots is not None:
                    facing = other[(entry >> back) & 15].astype(F32)
                    dots[pl.ds(place, 1), :] = jnp.sum(facing * prod, axis=0, keepdims=True)
            prefix[trip * (UNROLL // ROUND) + j + 1] = total


def at_step(ref, k):
    return lambda: ref.at[k]


def reduce_rows(net, at, block, chip, total, s):
    order = (2, 1, 3, 0)
    made = {}
    for k in order:
        for h in range(2):
            encode(s["core_s"].at[k, h], block(at.ys[k], at.far_core, h))
    for k in order:
        made[k] = net.copy(at_step(s["core_s"], k), at_step(s["core_r"], k), at.other)
    for k in order:
        for h in range(2):
            chip[k, h] = block(at.ys[k], at.core, h)
    yield 1
    sent = {}
    for k in order:
        made[k].wait_recv()
    for k in order:
        for h in range(2):
            value = chip[k, h] + decode(s["core_r"].at[k, h])
            if k:
                encode(s["y_s"].at[k, h], value)
            else:
                chip[0, h] = value
    for k in (2, 1, 3):
        sent[k] = net.copy(at_step(s["y_s"], k), at_step(s["y_r"], k), at.dy[k])
    yield 1
    for k in (1, 3, 2):
        sent[k].wait_recv()
    for h in range(2):
        value = chip[0, h]
        for k in (1, 3, 2):
            value = value + decode(s["y_r"].at[k, h])
        chip[0, h] = value
    encode(s["x_s"], chip[0, at.far_t])
    yield from swap(net, s["x_s"], s["x_r"], at.pair)
    total[...] = chip[0, at.t] + decode(s["x_r"])


def reduce_cols(net, at, block, here, total, s):
    order = (2, 1, 3, 0)
    ways = ((at.dx, at.dz), (at.dz, at.dx))
    part = (lambda k, j: block(k, j, 0), lambda k, j: block(j, k, 1))
    s1, r1 = (s["s10"], s["s11"]), (s["r10"], s["r11"])
    s2, r2 = (s["s20"], s["s21"]), (s["r20"], s["r21"])
    made, sent = {}, {}
    for k in order:
        for j in (2, 1, 3):
            for h in range(2):
                encode(s1[h].at[k, j], part[h](k, j))
        for j in (2, 1, 3):
            for h in range(2):
                made[h, k, j] = net.copy(s1[h].at[k, j], r1[h].at[k, j], ways[h][0][j])
        yield 1
    for k in order:
        for j in (1, 3, 2):
            for h in range(2):
                made[h, k, j].wait_recv()
        for h in range(2):
            value = part[h](k, 0)
            for j in (1, 3, 2):
                value = value + decode(r1[h].at[k, j])
            if k:
                encode(s2[h].at[k], value)
            else:
                here[h] = value
        for h in range(2):
            if k:
                sent[h, k] = net.copy(s2[h].at[k], r2[h].at[k], ways[h][1][k])
        yield 1
    for k in (2, 1, 3):
        for h in range(2):
            sent[h, k].wait_recv()
    for h in range(2):
        value = here[h]
        for k in (2, 1, 3):
            value = value + decode(r2[h].at[k])
        total[:, 128 * h : 128 * h + 128] = value


def sum_four(ref):
    return (ref[0] + ref[1]) + (ref[2] + ref[3])


def gram_rows(net, at, whole, four, two, full):
    block = (at.y * 4 + at.core * 2 + at.t) * 16
    four[at.z] = whole[pl.ds(pl.multiple_of(block, 16), 16), :]
    yield from spread(net, lambda p: four.at[p], at.z, at.dz[1:])
    two[0] = sum_four(four)
    yield from swap(net, at_step(two, 0), at_step(two, 1), at.dx[2])
    full[at.y, at.core, at.t] = two[0] + two[1]
    yield from spread(net, lambda p: full.at[p, at.core, at.t], at.y, at.dy[1:])
    column = lambda: full.at[:, at.core, at.t]
    yield from swap(net, column, column, at.pair)
    yield from swap(net, lambda: full.at[:, at.core], lambda: full.at[:, at.core], at.other)


def gram_cols(net, at, whole, four, two, full):
    block = (at.z * 4 + at.x) * 16
    four[at.y] = whole[pl.ds(pl.multiple_of(block, 16), 16), :]
    yield from spread(net, lambda p: four.at[p], at.y, at.dy[1:])
    two[0] = sum_four(four)
    yield from swap(net, at_step(two, 0), at_step(two, 1), at.other)
    full[at.z, at.x] = two[0] + two[1]
    yield from spread(net, lambda p: full.at[at.z, p], at.x, at.dx[1:])
    yield from spread(net, lambda p: full.at[p], at.z, at.dz[1:])


def reduce_time(net, at, part, two_x, four_z, two_c, four_y, total):
    two_x[0] = part[...]
    yield from swap(net, at_step(two_x, 0), at_step(two_x, 1), at.dx[2])
    four_z[at.z] = two_x[0] + two_x[1]
    yield from spread(net, lambda p: four_z.at[p], at.z, at.dz[1:])
    two_c[0] = sum_four(four_z)
    yield from swap(net, at_step(two_c, 0), at_step(two_c, 1), at.other)
    four_y[at.y] = two_c[0] + two_c[1]
    yield from spread(net, lambda p: four_y.at[p], at.y, at.dy[1:])
    total[...] = sum_four(four_y)


def exact_dot(left, right):
    high = right.astype(BF16)
    rest = right - high.astype(F32)
    mid = rest.astype(BF16)
    low = (rest - mid.astype(F32)).astype(BF16)
    return (
        jnp.dot(left, low, preferred_element_type=F32)
        + jnp.dot(left, mid, preferred_element_type=F32)
        + jnp.dot(left, high, preferred_element_type=F32)
    )


def gram(ref):
    block = ref[...]
    return lax.dot_general(block, block, (((0,), (0,)), ((), ())), preferred_element_type=F32)


def gradient_kernel(
    coords, count, values, rows, cols, times, grad_a, grad_b, grad_c, s, plan, send, recv, local
):
    at = Place()
    at.greet()
    net = Net(send, recv)
    a_full, b_full, c_full = s["a"], s["b"], s["c"]
    a_flat = a_full.reshape(16, EDGE, RANK)
    b_flat = b_full.reshape(16, EDGE, RANK)
    held, prefix = s["held"], s["prefix"]
    own = [
        pltpu.make_async_copy(cols.at[0], b_full.at[at.z, at.x], local.at[0]),
        pltpu.make_async_copy(rows.at[0], a_full.at[at.y, at.core, at.t], local.at[1]),
        pltpu.make_async_copy(times, c_full.at[at.t], local.at[2]),
        pltpu.make_async_copy(coords, s["coords"], local.at[3]),
    ]
    for copy in own:
        copy.start()
    part = SLOTS // LOADS
    loads = [
        pltpu.make_async_copy(
            values.at[part * i : part * i + part], held.at[part * i : part * i + part], local.at[4 + i]
        )
        for i in range(LOADS)
    ]
    at.await_all()
    bring_b = gather_cols(net, at, b_full, cols.at[0])
    bring_a = gather_rows(net, at, a_full, rows.at[0])
    bring_c = swap(net, times, c_full.at[at.t], at.pair)
    step(bring_a, bring_b, bring_c)
    for copy in loads:
        copy.start()
    for copy in own:
        copy.wait()

    step(bring_a, bring_b)
    s["times"][0:32] = jnp.zeros((32, RANK), F32)
    s["times"][32:64] = c_full[at.t].astype(F32)
    prefix[0] = jnp.zeros((EDGE, RANK), F32)
    s["dots"][PADDED:LANES] = jnp.zeros((LANES - PADDED, RANK), F32)
    for line in (1, 4, 6):
        s["plan"][line : line + 2] = jnp.zeros((2, LANES), jnp.int32)
    make_plan(s["plan"], s["coords"], count[0])
    tell = pltpu.make_async_copy(s["plan"], plan, local.at[4 + LOADS])
    tell.start()
    step(bring_a)
    tell.wait()
    for copy in loads:
        copy.wait()
    drive(bring_b, bring_c)
    s["gram"][...] = gram(b_full.reshape(16 * EDGE, RANK))
    share_b = gram_cols(net, at, s["gram"], s["gb4"], s["gb2"], s["gb"])
    step(share_b)
    drive(bring_a)
    share_a = gram_rows(net, at, s["gram_a"], s["ga4"], s["ga2"], s["ga"])

    def start_a():
        s["gram_a"][...] = gram(a_full.reshape(16 * EDGE, RANK))
        step(share_a)

    hooks = {0: start_a, 3: lambda: step(share_b, share_a), 4: lambda: step(share_b)}
    tile_pass(
        plan, 0, held, s["times"], b_flat, False, prefix, hooks, a_flat, s["dots"]
    )

    def row_block(y, core, t):
        i = y * 4 + core * 2 + t
        return prefix[plan[2, i]] - prefix[plan[1, i]]

    part_a = reduce_rows(net, at, row_block, s["chip"], s["total_a"], s)
    step(part_a)
    snaps = s["plan"][0:1] >> 17
    pick = (snaps == iota((32, LANES), 0) + 32).astype(F32).astype(BF16)
    s["part_c"][...] = exact_dot(pick, s["dots"][...])
    part_c = reduce_time(
        net, at, s["part_c"], s["cx2"], s["cz4"], s["cc2"], s["cy4"], s["total_c"]
    )
    step(part_c)
    hooks = {
        1: lambda: step(share_a, share_b),
        2: lambda: step(part_a, part_c),
        3: lambda: step(share_a),
    }
    tile_pass(plan, 3, held, s["times"], a_flat, True, prefix, hooks)

    def col_block(z, x, h):
        i = at.zs[z] * 4 + at.xs[x]
        lanes = slice(128 * h, 128 * h + 128)
        return prefix[plan[5, i], :, lanes] - prefix[plan[4, i], :, lanes]

    part_b = reduce_cols(net, at, col_block, s["here"], s["total_b"], s)
    step(share_b, share_a, part_c)
    for _ in range(4):
        step(part_b)
    step(share_a, part_c)
    whole_a = s["ga"][...].reshape(RANK, RANK)
    whole_b = s["gb"][...].reshape(RANK, RANK)
    whole_c = gram(c_full.reshape(64, RANK))
    s["near_a"][...] = exact_dot(a_full[at.y, at.core, at.t], whole_b * whole_c)
    s["near_b"][...] = exact_dot(b_full[at.z, at.x], whole_a * whole_c)
    step(part_b)
    step(part_a)
    for _ in range(2):
        step(part_b)
    step(part_c)
    s["out_c"][...] = exact_dot(c_full[at.t], whole_a * whole_b) - s["total_c"][...]
    gone_c = pltpu.make_async_copy(s["out_c"], grad_c, local.at[0])
    gone_c.start()
    step(part_b)
    step(part_a)
    s["near_a"][...] = s["near_a"][...] - s["total_a"][...]
    gone_a = pltpu.make_async_copy(s["near_a"], grad_a.at[0], local.at[1])
    gone_a.start()
    drive(part_b)
    s["near_b"][...] = s["near_b"][...] - s["total_b"][...]
    gone_b = pltpu.make_async_copy(s["near_b"], grad_b.at[0], local.at[2])
    gone_b.start()
    net.close()
    for copy in (gone_a, gone_b, gone_c):
        copy.wait()


def hand_over(in_a, in_b, in_c, out_a, out_b, out_c, held_a, held_b, held_c, sems):
    path = ((in_a, held_a, out_a), (in_b, held_b, out_b), (in_c, held_c, out_c))
    bring = [pltpu.make_async_copy(p[0], p[1], sems.at[i]) for i, p in enumerate(path)]
    leave = [pltpu.make_async_copy(p[1], p[2], sems.at[3 + i]) for i, p in enumerate(path)]
    for copy in bring:
        copy.start()
    for came, gone in zip(bring, leave):
        came.wait()
        gone.start()
    for copy in leave:
        copy.wait()


def on_device(tile_values, tile_coords, tile_counts, factor_rows, factor_cols, factor_time):
    values = tile_values.reshape(SLOTS, EDGE, EDGE)
    coords = tile_coords.reshape(3, 1, SLOTS)
    count = tile_counts.reshape(1)
    wire = lambda *lead: pltpu.VMEM(lead + (RANK,), I16)
    half = lambda *lead: pltpu.VMEM(lead + (EDGE,), I16)
    real = lambda *lead: pltpu.VMEM(lead + (RANK,), F32)
    big = EDGE + PAD
    scratch = dict(
        a=pltpu.VMEM((4, 2, 2, EDGE, RANK), BF16),
        b=pltpu.VMEM((4, 4, EDGE, RANK), BF16),
        c=pltpu.VMEM((2, 32, RANK), BF16),
        held=pltpu.VMEM((SLOTS, EDGE, EDGE), BF16),
        prefix=real(ROUNDS + 1, EDGE),
        dots=real(LANES), times=real(64), part_c=real(32),
        plan=pltpu.VMEM((8, LANES), jnp.int32), coords=pltpu.VMEM((3, 1, SLOTS), jnp.int32),
        chip=real(4, 2, EDGE), total_a=real(EDGE), total_b=real(EDGE), total_c=real(32),
        core_s=wire(4, 2, big), core_r=wire(4, 2, big),
        y_s=wire(4, 2, big), y_r=wire(4, 2, big), x_s=wire(big), x_r=wire(big),
        s10=half(4, 4, big), r10=half(4, 4, big), s20=half(4, big), r20=half(4, big),
        s11=half(4, 4, big), r11=half(4, 4, big), s21=half(4, big), r21=half(4, big),
        here=pltpu.VMEM((2, EDGE, EDGE), F32),
        gram=real(RANK), gram_a=real(RANK), near_a=real(EDGE), near_b=real(EDGE), out_c=real(32),
        ga4=real(4, 16), ga2=real(2, 16), ga=real(4, 2, 2, 16),
        gb4=real(4, 16), gb2=real(2, 16), gb=real(4, 4, 16),
        cx2=real(2, 32), cz4=real(4, 32), cc2=real(2, 32), cy4=real(4, 32),
    )
    smem = pl.BlockSpec(memory_space=pltpu.SMEM)
    anywhere = pl.BlockSpec(memory_space=pl.ANY)
    shapes = (
        jax.ShapeDtypeStruct((1, EDGE, RANK), F32),
        jax.ShapeDtypeStruct((1, EDGE, RANK), F32),
        jax.ShapeDtypeStruct((32, RANK), F32),
    )
    copies = 128
    grads = pl.pallas_call(
        gradient_kernel,
        out_shape=shapes,
        in_specs=[anywhere, smem] + [anywhere] * 4,
        out_specs=(anywhere,) * 3,
        scratch_shapes=[
            scratch,
            pltpu.SMEM((8, LANES), jnp.int32),
            pltpu.SemaphoreType.DMA((copies,)),
            pltpu.SemaphoreType.DMA((copies,)),
            pltpu.SemaphoreType.DMA((5 + LOADS,)),
        ],
        compiler_params=pltpu.CompilerParams(
            collective_id=0, has_side_effects=True, vmem_limit_bytes=60 << 20
        ),
        name="gradient",
    )(coords, count, values, factor_rows, factor_cols, factor_time)
    return pl.pallas_call(
        hand_over,
        out_shape=shapes,
        in_specs=[anywhere] * 3,
        out_specs=(anywhere,) * 3,
        scratch_shapes=[pltpu.VMEM(kind.shape, F32) for kind in shapes]
        + [pltpu.SemaphoreType.DMA((6,))],
        compiler_params=pltpu.CompilerParams(vmem_limit_bytes=60 << 20),
        name="hand_over",
    )(*grads)


def solution(mesh):
    return jax.shard_map(
        on_device,
        mesh=mesh,
        in_specs=(
            P("row", "col", "tm", None, None, None),
            P("row", "col", "tm", None, None),
            P("row", "col", "tm"),
            P("row", ("col", "tm"), None),
            P("col", ("row", "tm"), None),
            P("tm", None),
        ),
        out_specs=(P("row", ("col", "tm"), None), P("col", ("row", "tm"), None), P("tm", None)),
        check_vma=False,
    )
```
